256 devices in a mesh: cam: 8 (over x_hi, y), seq: 32 (over z, x_lo, core).
Axes of the slice: x: 4 (x_hi: 2, x_lo: 2; x = x_hi * 2 + x_lo), y: 4, z: 8, core: 2. Of those that a mesh axis runs over, the one named last changes fastest.
Arguments:
- q_tok: bfloat16 [8, 4096, 1536], P('cam', 'seq')
- k_tok: bfloat16 [8, 4096, 1536], P('cam', 'seq')
- v_tok: bfloat16 [8, 4096, 1536], P('cam', 'seq'), may hold values from -6 to 6
- strip_kv: bfloat16 [8, 2, 2, 1024, 1536], P('cam', None, None, 'seq')
- bev_keys: bfloat16 [32768, 1536], P(('cam', 'seq'))
- bev_values: bfloat16 [32768, 1536], P(('cam', 'seq')), may hold values from -6 to 6
- bev_list: int32 [8, 32, 3], P('cam', 'seq'), may hold values from 0 to 7, as said below
- bev_count: int32 [8, 32], P('cam', 'seq'), may hold values from 1 to 3, as said below
- gate_table: float32 [50, 3, 1536], replicated, may hold values from 0.1 to 1.9
- timestep: int32 [1], replicated, may hold values from 0 to 49
Outputs:
- blended: bfloat16 [8, 4096, 1536], P('cam', 'seq')
The draws below stay inside these ranges and needn't reach their ends.
Inputs may be any that keep to these rules, and one draw needn't show every extreme that they name: The 3 entries of each row of bev_list are different cameras. `bev_count`: some token block uses all 3 entries.
All inputs are finite; a program needn't handle non-finite values.
Results may differ from the reference program's by a relative error of at most 0.0039.
Values may be sent and summed in bfloat16 or wider, within the bound.
No kernel may reach another device: no remote copies, remote signals or barrier semaphores. Data moves between devices by JAX's collectives and lax.ppermute only.
A program may use at most 128 MiB of HBM per device.

```python
import math
import jax
import jax.numpy as jnp
from jax import lax

D = 1536
HEADS = 24
TOK_DEV = 128
EDGE_DEV = 32
BEV_DEV = 128
LIST = 3
NSTEP = 50
CAMS = 8
BLOCKS = 32
SEQ_TOK = 4096
EDGE = 1024
BEV = 32768


def draw_q_tok(key, part):
    key = jax.random.fold_in(key, 11)
    shape = (CAMS, SEQ_TOK, D)
    base = 2.0 * jnp.clip(jax.random.normal(key, shape, jnp.float32), -4.0, 4.0)
    return base.astype(jnp.bfloat16)


def draw_k_tok(key, part):
    key = jax.random.fold_in(key, 12)
    shape = (CAMS, SEQ_TOK, D)
    base = jnp.clip(jax.random.normal(key, shape, jnp.float32), -4.0, 4.0)
    return base.astype(jnp.bfloat16)


def draw_strip_kv(key, part):
    key = jax.random.fold_in(key, 13)
    shape = (CAMS, 2, 2, EDGE, D)
    base = jnp.clip(jax.random.normal(key, shape, jnp.float32), -4.0, 4.0)
    return base.astype(jnp.bfloat16)


def draw_bev_keys(key, part):
    key = jax.random.fold_in(key, 14)
    shape = (BEV, D)
    base = jnp.clip(jax.random.normal(key, shape, jnp.float32), -4.0, 4.0)
    return base.astype(jnp.bfloat16)


def draw_bev_list(key, part):
    key = jax.random.fold_in(key, 21)
    scores = jax.random.randint(key, (CAMS, BLOCKS, CAMS), 0, 1 << 20) * CAMS + jnp.arange(CAMS, dtype=jnp.int32)
    order = jnp.argsort(scores, axis=-1, stable=True)
    return order[:, :, :LIST].astype(jnp.int32)


def draw_bev_count(key, part):
    key = jax.random.fold_in(key, 22)
    counts = jax.random.randint(key, (CAMS, BLOCKS), 1, LIST + 1)
    return counts.at[0, 0].set(LIST).astype(jnp.int32)


def block_levels(stream_key, extent, split, smallest, high):
    loudness = 1.0
    for position, blocks in split:
        steps = jax.random.uniform(jax.random.fold_in(jax.random.fold_in(stream_key, 6), position), (blocks,), jnp.float32, smallest / len(split), high / len(split))
        loudness = loudness * jnp.repeat(jnp.exp(steps), extent[position] // blocks).reshape((-1,) + (1,) * (len(extent) - 1 - position))
    return loudness


def normal_values(rng, extent, scale, reach, pieces=(), held_as=jnp.bfloat16):
    factor_of = block_levels(rng, extent, pieces, -0.22, 0.18) if pieces else 1.0
    array = jax.random.normal(rng, extent, jnp.float32) * scale * factor_of
    return jnp.minimum(jnp.maximum(array, -reach), reach).astype(held_as)


def setup_inputs(seed: int = 0) -> dict:
    streams_of = jax.random.split(jax.random.key(seed), 11)
    q_tok = draw_q_tok(jax.random.fold_in(streams_of[10], 71), 0)
    k_tok = draw_k_tok(jax.random.fold_in(streams_of[10], 71), 0)
    v_tok = normal_values(streams_of[2], (CAMS, SEQ_TOK, D), 1.0, 6.0, ((0, 8), (1, 32)))
    strip_kv = draw_strip_kv(jax.random.fold_in(streams_of[10], 71), 0)
    bev_keys = draw_bev_keys(jax.random.fold_in(streams_of[10], 71), 0)
    bev_values = normal_values(streams_of[5], (BEV, D), 1.0, 6.0, ((0, 256),))
    bev_list = draw_bev_list(jax.random.fold_in(streams_of[10], 71), 0)
    bev_count = draw_bev_count(jax.random.fold_in(streams_of[10], 71), 0)
    gate_table = jnp.clip(1.0 + 0.18 * jax.random.normal(streams_of[8], (NSTEP, 3, D), jnp.float32), 0.1, 1.9)
    timestep = jax.random.randint(streams_of[9], (1,), 0, NSTEP).astype(jnp.int32)
    return {"q_tok": q_tok, "k_tok": k_tok, "v_tok": v_tok, "strip_kv": strip_kv, "bev_keys": bev_keys, "bev_values": bev_values, "bev_list": bev_list, "bev_count": bev_count, "gate_table": gate_table, "timestep": timestep}


def attend(queries, key_rows, value_rows, allowed):
    row_count = queries.shape[0]
    head_size = D // HEADS
    q_heads = queries.astype(jnp.float32).reshape(row_count, HEADS, head_size)
    k_heads = key_rows.astype(jnp.float32).reshape(key_rows.shape[0], HEADS, head_size)
    v_heads = value_rows.astype(jnp.float32).reshape(value_rows.shape[0], HEADS, head_size)
    scores = jnp.einsum('thd,rhd->htr', q_heads, k_heads) * (1.0 / math.sqrt(head_size))
    if allowed is not None:
        scores = jnp.where(allowed, scores, -1e+30)
    largest = lax.optimization_barrier(jnp.max(scores, axis=-1, keepdims=True))
    expons = jnp.exp(scores - largest)
    if allowed is not None:
        expons = jnp.where(allowed, expons, 0.0)
    weights = lax.optimization_barrier(expons.astype(jnp.bfloat16)).astype(jnp.float32)
    totals = lax.optimization_barrier(jnp.sum(expons, axis=-1))
    output = jnp.einsum('htr,rhd->thd', weights, v_heads) / jnp.transpose(totals)[:, :, None]
    return output.reshape(row_count, D)

def reference(q_tok, k_tok, v_tok, strip_kv, bev_keys, bev_values, bev_list, bev_count, gate_table, timestep):
    q_block = math.gcd(SEQ_TOK, 512)

    def one_camera(arrays):
        queries, key_rows, value_rows = arrays
        grouped = queries.reshape(SEQ_TOK // q_block, q_block, D)
        result = lax.map(lambda piece: attend(piece, key_rows, value_rows, None), grouped)
        return result.reshape(SEQ_TOK, D)
    self_out = lax.map(one_camera, (q_tok, k_tok, v_tok))
    from_left = jnp.roll(strip_kv[:, 1], 1, axis=0)
    from_right = jnp.roll(strip_kv[:, 0], -1, axis=0)
    view_keys = jnp.concatenate([from_left[:, 0].reshape(CAMS, BLOCKS, EDGE_DEV, D), from_right[:, 0].reshape(CAMS, BLOCKS, EDGE_DEV, D)], axis=2)
    view_values = jnp.concatenate([from_left[:, 1].reshape(CAMS, BLOCKS, EDGE_DEV, D), from_right[:, 1].reshape(CAMS, BLOCKS, EDGE_DEV, D)], axis=2)
    q_blocks = q_tok.reshape(CAMS, BLOCKS, TOK_DEV, D)

    def view_camera(arrays):
        queries, key_rows, value_rows = arrays
        return jax.vmap(lambda qq, kk, vv: attend(qq, kk, vv, None))(queries, key_rows, value_rows)
    view_out = lax.map(view_camera, (q_blocks, view_keys, view_values)).reshape(CAMS, SEQ_TOK, D)
    bev_k = bev_keys.reshape(CAMS, BLOCKS, BEV_DEV, D)
    bev_v = bev_values.reshape(CAMS, BLOCKS, BEV_DEV, D)
    block_ids = jnp.arange(BLOCKS, dtype=jnp.int32)[:, None]

    def bev_camera(arrays):
        queries, listed, counts = arrays
        key_rows = bev_k[listed, block_ids].reshape(BLOCKS, LIST * BEV_DEV, D)
        value_rows = bev_v[listed, block_ids].reshape(BLOCKS, LIST * BEV_DEV, D)
        slot_of = jnp.arange(LIST * BEV_DEV, dtype=jnp.int32) // BEV_DEV
        allowed = slot_of[None, :] < counts[:, None]
        return jax.vmap(lambda qq, kk, vv, aa: attend(qq, kk, vv, aa[None, None, :]))(queries, key_rows, value_rows, allowed)
    bev_out = lax.map(bev_camera, (q_blocks, bev_list, bev_count)).reshape(CAMS, SEQ_TOK, D)
    onehot = (jnp.arange(NSTEP, dtype=jnp.int32) == timestep[0]).astype(jnp.float32)
    gate_rows = jnp.tensordot(onehot, gate_table, axes=1, precision=lax.Precision.HIGHEST)
    blended = gate_rows[0] * self_out + gate_rows[1] * view_out + gate_rows[2] * bev_out
    return blended.astype(jnp.bfloat16)
```

```python
import functools
import math

import jax
import jax.numpy as jnp
from jax import lax
from jax.experimental import pallas as pl
from jax.experimental.pallas import tpu as pltpu
from jax.sharding import PartitionSpec as P

BF = jnp.bfloat16
F32 = jnp.float32
LANES = 128
HALF = 64
LIST = 3
NZ = 8
NY = 4
TOK = 128
WIDTH = 1536
PAIRS = WIDTH // LANES
GROUP_PAIRS = PAIRS // NY
GROUP_COLS = GROUP_PAIRS * LANES
KV_ROWS = 3 * TOK
Q_ROWS = TOK + TOK // 2
KEYS = 4096
BQ = 256
KT = 256
SCALE = math.log2(math.e) / math.sqrt(HALF)
NT = (((1,), (1,)), ((), ()))
VMEM_LIMIT = 56 * 2**20

NEAR = (0, 1, 7, 2)
FAR = (6, 3, 5, 4)


def along_z(by):
    return [(4 * z + r, 4 * ((z + by) % NZ) + r) for z in range(NZ) for r in range(4)]


def other_place(x_lo, core):
    return [(s, s ^ (2 * x_lo + core)) for s in range(4 * NZ)]


def along_cam(x_hi, y):
    return [(NY * a + b, NY * ((a + x_hi) % 2) + (b + y) % NY) for a in range(2) for b in range(NY)]


def ring_cam(by):
    return [(c, (c + by) % (2 * NY)) for c in range(2 * NY)]


def low_lanes(rows):
    return lax.broadcasted_iota(jnp.int32, (rows, LANES), 1) < HALF


def lane_tile(ref, index):
    return ref[:, pl.ds(pl.multiple_of(index * LANES, LANES), LANES)]


def turned(x, flag):
    return jnp.where(flag, pltpu.roll(x, HALF, 1), x)


def params():
    return pltpu.CompilerParams(vmem_limit_bytes=VMEM_LIMIT)


def pack_z_kernel(q_ref, k_ref, v_ref, *outs):
    z = lax.axis_index("seq") // 4
    low = low_lanes(TOK)
    low_half = low_lanes(TOK // 2)
    for d in range(NZ):
        g = lax.rem(z + d, NZ)
        odd = lax.rem(g, 2) == 1
        tile = NZ + g // 2
        kv_out, q_out = outs[d], outs[NZ + d]
        kv_out[0:TOK] = lane_tile(k_ref, g)
        kv_out[TOK : 2 * TOK] = lane_tile(v_ref, g)
        k_one = turned(lane_tile(k_ref, tile), odd)
        v_one = turned(lane_tile(v_ref, tile), jnp.logical_not(odd))
        kv_out[2 * TOK :] = jnp.where(low, k_one, v_one)
        q_out[0:TOK] = lane_tile(q_ref, g)
        q_one = lane_tile(q_ref, tile)
        q_first = turned(q_one[: TOK // 2], odd)
        q_second = turned(q_one[TOK // 2 :], jnp.logical_not(odd))
        q_out[TOK:] = jnp.where(low_half, q_first, q_second)


def pack_y_kernel(q_ref, k_ref, v_ref, *outs):
    y = lax.rem(lax.axis_index("cam"), NY)
    for d in range(NY):
        g = lax.rem(y + d, NY)
        cols = pl.ds(pl.multiple_of(g * GROUP_COLS, LANES), GROUP_COLS)
        outs[d][0:TOK] = q_ref[:, cols]
        outs[NY + d][0:TOK] = k_ref[:, cols]
        outs[NY + d][TOK:] = v_ref[:, cols]


def self_kernel(*refs):
    kv_refs, q_refs, o_refs = refs[:8], refs[8:16], refs[16:24]
    k_all, v_all, q_all, s_buf, m_buf, o_all = refs[24:]
    at = 0
    for ref in kv_refs:
        for i in range(4):
            rows = slice(at, at + TOK)
            base = i * KV_ROWS
            one = ref[base + 2 * TOK : base + 3 * TOK]
            k_all[0, rows] = ref[base : base + TOK]
            k_all[1, rows] = one
            v_all[0, rows, :LANES] = ref[base + TOK : base + 2 * TOK]
            v_all[1, rows, :LANES] = one
            at += TOK
    v_all[:, :, LANES:] = jnp.ones((2, KEYS, LANES), BF)
    low, low_half = low_lanes(TOK), low_lanes(TOK // 2)
    nil, nil_half = jnp.zeros((TOK, LANES), BF), jnp.zeros((TOK // 2, LANES), BF)
    for d in range(NZ):
        q = q_refs[d][0:TOK]
        q_one = q_refs[d][TOK:]
        rows = slice(d * TOK, (d + 1) * TOK)
        q_all[0, rows] = jnp.where(low, q, nil)
        q_all[1, rows] = jnp.where(low, nil, q)
        q_all[2, d * TOK : d * TOK + TOK // 2] = jnp.where(low_half, q_one, nil_half)
        q_all[2, d * TOK + TOK // 2 : (d + 1) * TOK] = jnp.where(
            low_half, pltpu.roll(q_one, HALF, 1), nil_half
        )
    blocks = NZ * TOK // BQ
    steps = 3 * blocks

    def scores(i, slot):
        h = i // blocks
        start = pl.multiple_of(lax.rem(i, blocks) * BQ, BQ)
        q = q_all[h, pl.ds(start, BQ)]
        largest = jnp.full((BQ, LANES), -jnp.inf, F32)
        for t in range(KEYS // KT):
            s = lax.dot_general(
                q, k_all[h // 2, t * KT : (t + 1) * KT], NT, preferred_element_type=F32
            )
            s_buf[slot, :, t * KT : (t + 1) * KT] = s
            for j in range(KT // LANES):
                largest = jnp.maximum(largest, s[:, j * LANES : (j + 1) * LANES])
        top = jnp.max(largest, axis=1, keepdims=True) * SCALE
        m_buf[slot] = jnp.broadcast_to(top, (BQ, LANES))

    def values(i, slot):
        h = i // blocks
        start = pl.multiple_of(lax.rem(i, blocks) * BQ, BQ)
        top = jnp.concatenate([m_buf[slot]] * (KT // LANES), axis=1)
        total = jnp.zeros((BQ, 2 * LANES), F32)
        for t in range(KEYS // KT):
            s = s_buf[slot, :, t * KT : (t + 1) * KT]
            w = jnp.exp2(s * SCALE - top).astype(BF)
            total = total + jnp.dot(
                w, v_all[h // 2, t * KT : (t + 1) * KT], preferred_element_type=F32
            )
        o_all[h, pl.ds(start, BQ)] = total[:, :LANES] / total[:, LANES:]

    scores(0, 0)

    def two_steps(j, carry):
        i = 2 * j
        scores(i + 1, 1)
        values(i, 0)
        scores(jnp.minimum(i + 2, steps - 1), 0)
        values(i + 1, 1)
        return carry

    lax.fori_loop(0, steps // 2, two_steps, 0)
    for d in range(NZ):
        rows = slice(d * TOK, (d + 1) * TOK)
        o_refs[d][0:TOK] = jnp.where(low, o_all[0, rows], o_all[1, rows]).astype(BF)
        first = o_all[2, d * TOK : d * TOK + TOK // 2]
        second = o_all[2, d * TOK + TOK // 2 : (d + 1) * TOK]
        o_refs[d][TOK:] = jnp.where(low_half, pltpu.roll(first, HALF, 1), second).astype(BF)


def pair_attention(q, blocks, allowed=None):
    rows = q.shape[0]
    low = low_lanes(rows)
    nil = jnp.zeros_like(q)
    both = jnp.concatenate([jnp.where(low, q, nil), jnp.where(low, nil, q)], axis=0)
    scores = []
    for j, (keys, _) in enumerate(blocks):
        s = lax.dot_general(both, keys, NT, preferred_element_type=F32) * SCALE
        if allowed is not None:
            s = jnp.where(allowed[j], s, -1e30)
        scores.append(s)
    top = functools.reduce(jnp.maximum, [jnp.max(s, axis=1, keepdims=True) for s in scores])
    total = jnp.zeros((2 * rows, 2 * LANES), F32)
    for s, (_, vals) in zip(scores, blocks):
        w = jnp.exp2(s - top).astype(BF)
        wide = jnp.concatenate([vals, jnp.ones_like(vals)], axis=1)
        total = total + jnp.dot(w, wide, preferred_element_type=F32)
    out = total[:, :LANES] / total[:, LANES:]
    return jnp.where(low, out[:rows], out[rows:])


def view_kernel(q_ref, left_ref, right_ref, out_ref):
    for p in range(PAIRS):
        cols = slice(p * LANES, (p + 1) * LANES)
        keys = jnp.concatenate([left_ref[0, :, cols], right_ref[0, :, cols]], axis=0)
        vals = jnp.concatenate([left_ref[1, :, cols], right_ref[1, :, cols]], axis=0)
        out_ref[:, cols] = pair_attention(q_ref[:, cols], [(keys, vals)])


def bev_kernel(uses_ref, *refs):
    q_refs, kv_refs, far_ref, o_refs, kv_all = refs[:4], refs[4:8], refs[8], refs[9:13], refs[13]
    cam = lax.axis_index("cam")
    x_hi, y = cam // NY, lax.rem(cam, NY)
    for d in range(NY):
        kv_all[d] = kv_refs[d][...]
        kv_all[NY + d] = far_ref[d * 2 * TOK : (d + 1) * 2 * TOK]
    for d in range(NY):
        me = x_hi * NY + lax.rem(y - d + NY, NY)
        places, allowed = [], []
        for j in range(LIST):
            e = uses_ref[me, j]
            place = lax.rem(y - lax.rem(e, NY) + NY, NY)
            places.append(jnp.where(e // NY == x_hi, place, place + NY))
            allowed.append(j < uses_ref[me, LIST])
        for p in range(GROUP_PAIRS):
            cols = slice(p * LANES, (p + 1) * LANES)
            blocks = [
                (kv_all[at, 0:TOK, cols], kv_all[at, TOK : 2 * TOK, cols]) for at in places
            ]
            o_refs[d][:, cols] = pair_attention(q_refs[d][:, cols], blocks, allowed).astype(BF)


def blend_kernel(*refs):
    self_refs, bev_refs, view_ref, gain_ref = refs[:8], refs[8:12], refs[12], refs[13]
    out_ref, self_all, one_all, bev_all = refs[14:]
    z = lax.axis_index("seq") // 4
    y = lax.rem(lax.axis_index("cam"), NY)
    for d in range(NZ):
        g = lax.rem(z + d, NZ)
        self_all[g] = self_refs[d][0:TOK].astype(F32)
        one = self_refs[d][TOK:].astype(F32)
        one_all[g, 0 : TOK // 2] = one
        one_all[g, TOK // 2 :] = pltpu.roll(one, HALF, 1)
    for d in range(NY):
        bev_all[lax.rem(y + d, NY)] = bev_refs[d][...]
    low = low_lanes(TOK)
    for p in range(PAIRS):
        cols = slice(p * LANES, (p + 1) * LANES)
        if p < NZ:
            mine = self_all[p]
        else:
            first, second = one_all[2 * (p - NZ)], one_all[2 * (p - NZ) + 1]
            mine = jnp.where(low, first, pltpu.roll(second, HALF, 1))
        at = p % GROUP_PAIRS
        layout = bev_all[p // GROUP_PAIRS, :, at * LANES : (at + 1) * LANES].astype(F32)
        blended = gain_ref[0:1, cols] * mine + gain_ref[1:2, cols] * view_ref[:, cols]
        out_ref[:, cols] = (blended + gain_ref[2:3, cols] * layout).astype(BF)


def of(shape, dtype=BF):
    return jax.ShapeDtypeStruct(shape, dtype)


def cost(flops, moved, exps):
    return pl.CostEstimate(flops=flops, bytes_accessed=moved, transcendentals=exps)


def shards(
    q_tok, k_tok, v_tok, strip_kv, bev_keys, bev_values, bev_list, bev_count, gate_table, timestep
):
    q, k, v = q_tok[0], k_tok[0], v_tok[0]
    packed = pl.pallas_call(
        pack_z_kernel,
        out_shape=[of((KV_ROWS, LANES))] * NZ + [of((Q_ROWS, LANES))] * NZ,
        compiler_params=params(),
        cost_estimate=cost(0, 2 * 6 * TOK * WIDTH, 0),
        name="pack_z",
    )(q, k, v)
    kv_out, q_out = packed[:NZ], packed[NZ:]
    kv_in = [kv_out[0]] + [lax.ppermute(kv_out[d], "seq", along_z(d)) for d in range(1, NZ)]
    q_in = [q_out[0]] + [lax.ppermute(q_out[d], "seq", along_z(d)) for d in range(1, NZ)]
    kv_parts = []
    for ring in (NEAR, FAR):
        own = jnp.concatenate([kv_in[d] for d in ring], axis=0)
        beside = lax.ppermute(own, "seq", other_place(1, 0))
        kv_parts += [own, beside]
        kv_parts += [lax.ppermute(t, "seq", other_place(0, 1)) for t in (own, beside)]

    uses = jnp.concatenate([bev_list[0], bev_count], axis=1)
    uses = lax.all_gather(uses, "cam", axis=0, tiled=True)
    from_left = lax.ppermute(strip_kv[0, 1], "cam", ring_cam(1))
    from_right = lax.ppermute(strip_kv[0, 0], "cam", ring_cam(-1))
    view = pl.pallas_call(
        view_kernel,
        out_shape=of((TOK, WIDTH), F32),
        compiler_params=params(),
        cost_estimate=cost(TOK * 64 * WIDTH * 8, 4 * TOK * WIDTH, TOK * 64 * 24),
        name="view",
    )(q, from_left, from_right)

    packed = pl.pallas_call(
        pack_y_kernel,
        out_shape=[of((TOK, GROUP_COLS))] * NY + [of((2 * TOK, GROUP_COLS))] * NY,
        compiler_params=params(),
        cost_estimate=cost(0, 2 * 6 * TOK * WIDTH, 0),
        name="pack_y",
    )(q, bev_keys, bev_values)
    bev_q = [packed[0]] + [
        lax.ppermute(packed[d], "cam", along_cam(0, d)) for d in range(1, NY)
    ]
    bev_kv = [packed[NY]] + [
        lax.ppermute(packed[NY + d], "cam", along_cam(0, d)) for d in range(1, NY)
    ]
    bev_far = lax.ppermute(jnp.concatenate(bev_kv, axis=0), "cam", along_cam(1, 0))

    self_out = pl.pallas_call(
        self_kernel,
        out_shape=[of((Q_ROWS, LANES))] * NZ,
        scratch_shapes=[
            pltpu.VMEM((2, KEYS, LANES), BF),
            pltpu.VMEM((2, KEYS, 2 * LANES), BF),
            pltpu.VMEM((3, NZ * TOK, LANES), BF),
            pltpu.VMEM((2, BQ, KEYS), F32),
            pltpu.VMEM((2, BQ, LANES), F32),
            pltpu.VMEM((3, NZ * TOK, LANES), F32),
        ],
        compiler_params=params(),
        cost_estimate=cost(4 * 4 * TOK * KEYS * WIDTH, 4 * KEYS * 384, TOK * KEYS * 24),
        name="self_attention",
    )(*kv_parts, *q_in)
    bev_out = pl.pallas_call(
        bev_kernel,
        out_shape=[of((TOK, GROUP_COLS))] * NY,
        in_specs=[pl.BlockSpec(memory_space=pltpu.SMEM)]
        + [pl.BlockSpec(memory_space=pltpu.VMEM)] * 9,
        scratch_shapes=[pltpu.VMEM((2 * NY, 2 * TOK, GROUP_COLS), BF)],
        compiler_params=params(),
        cost_estimate=cost(4 * 4 * TOK * 384 * WIDTH, 4 * TOK * WIDTH, TOK * 384 * 24),
        name="layout_attention",
    )(uses, *bev_q, *bev_kv, bev_far)
    bev_in = [bev_out[0]] + [
        lax.ppermute(bev_out[d], "cam", along_cam(0, NY - d)) for d in range(1, NY)
    ]
    self_in = [self_out[0]] + [
        lax.ppermute(self_out[d], "seq", along_z(NZ - d)) for d in range(1, NZ)
    ]
    gains = lax.dynamic_index_in_dim(gate_table, timestep[0], 0, keepdims=False)
    blended = pl.pallas_call(
        blend_kernel,
        out_shape=of((TOK, WIDTH)),
        scratch_shapes=[
            pltpu.VMEM((NZ, TOK, LANES), F32),
            pltpu.VMEM((NZ, TOK, LANES), F32),
            pltpu.VMEM((NY, TOK, GROUP_COLS), BF),
        ],
        compiler_params=params(),
        cost_estimate=cost(0, 10 * TOK * WIDTH, 0),
        name="blend",
    )(*self_in, *bev_in, view, gains)
    return blended[None]


def solution(mesh):
    return jax.shard_map(
        shards,
        mesh=mesh,
        in_specs=(
            P("cam", "seq", None),
            P("cam", "seq", None),
            P("cam", "seq", None),
            P("cam", None, None, "seq", None),
            P(("cam", "seq"), None),
            P(("cam", "seq"), None),
            P("cam", "seq", None),
            P("cam", "seq"),
            P(),
            P(),
        ),
        out_specs=P("cam", "seq", None),
        check_vma=False,
    )
```

```python
import functools
import math

import jax
import jax.numpy as jnp
from jax import lax
from jax.experimental import pallas as pl
from jax.experimental.pallas import tpu as pltpu
from jax.sharding import PartitionSpec as P

BF = jnp.bfloat16
F32 = jnp.float32
LANES = 128
HALF = 64
LIST = 3
NZ = 8
CAMS = 8
NY = 4
AWAY = ((0, 0), (1, 0), (0, 1), (0, 3), (1, 1), (0, 2), (1, 3), (1, 2))
PLACES = 2 * NZ
TOK = 128
EDGE = 32
WIDTH = 1536
KEYS = 4096
META = 16
BQ = 256
KT = 256
SCALE = math.log2(math.e) / math.sqrt(HALF)
NT = (((1,), (1,)), ((), ()))
VMEM_LIMIT = 56 * 2**20

Q_ONE = TOK
KV_TWO = Q_ONE + TOK // 2
Q_TWO = KV_TWO + TOK
Z_ROWS = Q_TWO + TOK // 4
O_ROWS = TOK // 2 + TOK // 4

C_V = TOK
C_ONE = 2 * TOK
C_Q = 3 * TOK
C_QONE = 4 * TOK
C_STRIP = C_QONE + TOK // 2
C_META = C_STRIP + 6 * EDGE
C_ROWS = C_META + META
CO_ROWS = TOK + TOK // 2


def low_lanes(rows):
    return lax.broadcasted_iota(jnp.int32, (rows, LANES), 1) < HALF


def half_turn(x):
    return pltpu.roll(x, HALF, 1)


def side_by_side(a, a_half, b, b_half):
    left = half_turn(a) if a_half else a
    right = b if b_half else half_turn(b)
    return jnp.where(low_lanes(a.shape[0]), left, right)


def folded(x, half):
    n = x.shape[0] // 2
    return side_by_side(x[:n], half, x[n:], half)


def tile(ref, index):
    return ref[:, index * LANES : (index + 1) * LANES]


def tile_at(ref, index):
    return ref[:, pl.ds(pl.multiple_of(index * LANES, LANES), LANES)]


def turned(x, flag):
    return jnp.where(flag, half_turn(x), x)


def cam_away(place, sign):
    cam = lax.axis_index("cam")
    x_hi, y = AWAY[place]
    x_hi = lax.rem(cam // NY + x_hi, 2)
    return x_hi * NY + lax.rem(lax.rem(cam, NY) + (y if sign > 0 else NY - y), NY)


def params():
    return pltpu.CompilerParams(vmem_limit_bytes=VMEM_LIMIT)


def pack_z_kernel(q_ref, k_ref, v_ref, out_ref):
    for z in range(NZ):
        at, half = NZ + z // 2, z % 2
        shared = side_by_side(tile(k_ref, at), half, tile(v_ref, at), half)
        q_shared = tile(q_ref, at)
        k, v, q = tile(k_ref, z), tile(v_ref, z), tile(q_ref, z)
        for x in range(2):
            place = 2 * z + x
            out_ref[place, :Q_ONE] = side_by_side(k, x, v, x)
            out_ref[place, Q_ONE:KV_TWO] = folded(q, x)
            out_ref[place, KV_TWO:Q_TWO] = shared
            out_ref[place, Q_TWO:] = folded(q_shared[x * HALF : (x + 1) * HALF], half)


def pack_cam_kernel(list_ref, count_ref, q_ref, k_ref, v_ref, strip_ref, *outs):
    lane = lax.broadcasted_iota(jnp.int32, (META, LANES), 1)
    uses = jnp.where(lane == LIST, count_ref[0, 0], 0)
    for j in range(LIST):
        uses = jnp.where(lane == j, list_ref[0, 0, j], uses)
    uses = uses.astype(F32).astype(BF)
    low = low_lanes(TOK)
    for i, out_ref in enumerate(outs):
        p = cam_away(i, 1)
        at = CAMS + p // 2
        odd = lax.rem(p, 2) == 1
        even = jnp.logical_not(odd)

        def third(k, v):
            first = turned(tile_at(k, at), odd)
            return jnp.where(low[: first.shape[0]], first, turned(tile_at(v, at), even))

        out_ref[:C_V] = tile_at(k_ref, p)
        out_ref[C_V:C_ONE] = tile_at(v_ref, p)
        out_ref[C_ONE:C_Q] = third(k_ref, v_ref)
        out_ref[C_Q:C_QONE] = tile_at(q_ref, p)
        q = tile_at(q_ref, at)
        out_ref[C_QONE:C_STRIP] = jnp.where(
            low[:HALF], turned(q[:HALF], odd), turned(q[HALF:], even)
        )
        for side in range(2):
            base = C_STRIP + side * EDGE
            k, v = strip_ref.at[side, 0], strip_ref.at[side, 1]
            out_ref[base : base + EDGE] = tile_at(k, p)
            out_ref[base + 2 * EDGE : base + 3 * EDGE] = tile_at(v, p)
            out_ref[base + 4 * EDGE : base + 5 * EDGE] = third(k, v)
        out_ref[C_META:] = uses


def self_kernel(mine_ref, other_ref, o_ref, kv_all, q_all, s_buf, m_buf, o_all):
    ones = jnp.ones((TOK, LANES), BF)
    for i, ref in enumerate((mine_ref, other_ref)):
        for place in range(PLACES):
            at = (i * PLACES + place) * TOK
            rows = slice(at, at + TOK)
            kv_all[0, rows, :LANES] = ref[place, :Q_ONE]
            kv_all[0, rows, LANES:] = ones
            kv_all[1, rows, :LANES] = ref[place, KV_TWO:Q_TWO]
            kv_all[1, rows, LANES:] = ones

    def unfold(q, at):
        n = q.shape[0]
        low, nil = low_lanes(n), jnp.zeros((n, LANES), BF)
        q_all[at : at + n] = jnp.where(low, q, nil)
        q_all[at + n : at + 2 * n] = jnp.where(low, half_turn(q), nil)

    first = PLACES * TOK
    for place in range(PLACES):
        unfold(mine_ref[place, Q_ONE:KV_TWO], place * TOK)
        unfold(mine_ref[place, Q_TWO:], first + place * HALF)
    steps = 3 * first // 2 // BQ

    def scores(i, slot):
        h = i // (first // BQ)
        q = q_all[pl.ds(pl.multiple_of(i * BQ, BQ), BQ)]
        largest = jnp.full((BQ, LANES), -jnp.inf, F32)
        for t in range(KEYS // KT):
            keys = kv_all[h, t * KT : (t + 1) * KT, :LANES]
            s = lax.dot_general(q, keys, NT, preferred_element_type=F32)
            s_buf[slot, :, t * KT : (t + 1) * KT] = s
            for j in range(KT // LANES):
                largest = jnp.maximum(largest, s[:, j * LANES : (j + 1) * LANES])
        top = jnp.max(largest, axis=1, keepdims=True) * SCALE
        m_buf[slot] = jnp.broadcast_to(top, (BQ, LANES))

    def values(i, slot):
        h = i // (first // BQ)
        top = jnp.concatenate([m_buf[slot]] * (KT // LANES), axis=1)
        total = jnp.zeros((BQ, 2 * LANES), F32)
        for t in range(KEYS // KT):
            s = s_buf[slot, :, t * KT : (t + 1) * KT]
            w = jnp.exp2(s * SCALE - top).astype(BF)
            total = total + jnp.dot(
                w, kv_all[h, t * KT : (t + 1) * KT], preferred_element_type=F32
            )
        o_all[pl.ds(pl.multiple_of(i * BQ, BQ), BQ)] = total[:, :LANES] / total[:, LANES:]

    scores(0, 0)

    def two_steps(j, carry):
        i = 2 * j
        scores(i + 1, 1)
        values(i, 0)
        scores(jnp.minimum(i + 2, steps - 1), 0)
        values(i + 1, 1)
        return carry

    lax.fori_loop(0, steps // 2, two_steps, 0)
    for place in range(PLACES):
        at = place * TOK
        o_ref[place, : TOK // 2] = folded(o_all[at : at + TOK], 1).astype(BF)
        at = first + place * HALF
        o_ref[place, TOK // 2 :] = folded(o_all[at : at + HALF], 1).astype(BF)


def attention(q, blocks, allowed=None):
    scores = []
    for j, (keys, _) in enumerate(blocks):
        s = lax.dot_general(q, keys, NT, preferred_element_type=F32) * SCALE
        if allowed is not None:
            s = jnp.where(allowed[j], s, -1e30)
        scores.append(s)
    top = functools.reduce(jnp.maximum, [jnp.max(s, axis=1, keepdims=True) for s in scores])
    total = jnp.zeros((q.shape[0], 2 * LANES), F32)
    for s, (_, vals) in zip(scores, blocks):
        w = jnp.exp2(s - top).astype(BF)
        wide = jnp.concatenate([vals, jnp.ones_like(vals)], axis=1)
        total = total + jnp.dot(w, wide, preferred_element_type=F32)
    return total[:, :LANES] / total[:, LANES:]


def cam_kernel(*refs):
    in_refs, gain_ref, o_ref = refs[:CAMS], refs[CAMS], refs[CAMS + 1]
    got_ref, uses_vec, uses_ref = refs[CAMS + 2 :]
    p = lax.axis_index("cam")
    for i in range(CAMS):
        got_ref[cam_away(i, -1)] = in_refs[i][...]
    for c in range(CAMS):
        uses = got_ref[c, C_META:].astype(F32)[:1].astype(jnp.int32)
        uses_vec[c : c + 1] = uses
    pltpu.sync_copy(uses_vec, uses_ref)

    def gain(row):
        pair = gain_ref[row : row + 1, pl.ds(pl.multiple_of(p * LANES, LANES), LANES)]
        at = CAMS + p // 2
        one = gain_ref[row : row + 1, pl.ds(pl.multiple_of(at * LANES, LANES), LANES)]
        one = jnp.broadcast_to(one, (8, LANES))
        return pair, jnp.where(lax.rem(p, 2) == 1, one, half_turn(one))[:1]

    view_gain, bev_gain = gain(1), gain(2)
    low, nil = low_lanes(TOK), jnp.zeros((TOK, LANES), BF)
    low_half, nil_half = low_lanes(HALF), jnp.zeros((HALF, LANES), BF)
    for c in range(CAMS):
        listed = [uses_ref[c, j] for j in range(LIST)]
        allowed = [j < uses_ref[c, LIST] for j in range(LIST)]
        left, right = (c - 1) % CAMS, (c + 1) % CAMS
        ends = ((left, C_STRIP + EDGE), (right, C_STRIP))

        def strips(part):
            return jnp.concatenate(
                [got_ref[e, at + part : at + part + EDGE] for e, at in ends], axis=0
            )

        q = got_ref[c, C_Q:C_QONE]
        q = jnp.concatenate([jnp.where(low, q, nil), jnp.where(low, nil, q)], axis=0)
        view = attention(q, [(strips(0), strips(2 * EDGE))])
        blocks = [(got_ref[e, :C_V], got_ref[e, C_V:C_ONE]) for e in listed]
        bev = attention(q, blocks, allowed)
        out = view * view_gain[0] + bev * bev_gain[0]
        o_ref[c, :TOK] = jnp.where(low, out[:TOK], out[TOK:]).astype(BF)

        q = got_ref[c, C_QONE:C_STRIP]
        q = jnp.concatenate(
            [jnp.where(low_half, q, nil_half), jnp.where(low_half, half_turn(q), nil_half)], axis=0
        )
        both = strips(4 * EDGE)
        view = attention(q, [(both, both)])
        blocks = [(got_ref[e, C_ONE:C_Q], got_ref[e, C_ONE:C_Q]) for e in listed]
        bev = attention(q, blocks, allowed)
        out = view * view_gain[1] + bev * bev_gain[1]
        o_ref[c, TOK:] = folded(out, 1).astype(BF)


def blend_kernel(self_ref, cam_ref, gain_ref, out_ref):
    def unfolded(x, y, n):
        lower = side_by_side(x, 0, y, 0)
        upper = side_by_side(x, 1, y, 1)
        return jnp.concatenate([lower, upper], axis=0)

    for i in range(WIDTH // LANES):
        cols = slice(i * LANES, (i + 1) * LANES)
        if i < NZ:
            one, two = (self_ref[2 * i + x, : TOK // 2].astype(F32) for x in range(2))
            mine = unfolded(one, two, HALF)
            other = cam_ref[i, :TOK].astype(F32)
        else:
            z = 2 * (i - NZ)
            parts = []
            for x in range(2):
                one, two = (self_ref[2 * (z + k) + x, TOK // 2 :].astype(F32) for k in range(2))
                parts.append(unfolded(one, two, HALF // 2))
            mine = jnp.concatenate(parts, axis=0)
            one, two = (cam_ref[z + k, TOK:].astype(F32) for k in range(2))
            other = unfolded(one, two, HALF)
        out_ref[:, cols] = (gain_ref[0:1, cols] * mine + other).astype(BF)


def of(shape, dtype=BF):
    return jax.ShapeDtypeStruct(shape, dtype)


def cost(flops, moved, exps):
    return pl.CostEstimate(flops=flops, bytes_accessed=moved, transcendentals=exps)


def after(x, *done):
    return lax.optimization_barrier((x,) + done)[0]


SAME_CORE = [[4 * z + 2 * x + c for z in range(NZ) for x in range(2)] for c in range(2)]


def z_exchange(x):
    return lax.all_to_all(x, "seq", 0, 0, axis_index_groups=SAME_CORE, tiled=True)


def cam_exchange(x):
    return lax.all_to_all(x, "cam", 0, 0, tiled=True)


def shards(
    q_tok, k_tok, v_tok, strip_kv, bev_keys, bev_values, bev_list, bev_count, gate_table, timestep
):
    q, k, v = q_tok[0], k_tok[0], v_tok[0]
    smem = pl.BlockSpec(memory_space=pltpu.SMEM)
    vmem = pl.BlockSpec(memory_space=pltpu.VMEM)
    gains = lax.dynamic_index_in_dim(gate_table, timestep[0], 0, keepdims=False)
    to_z = pl.pallas_call(
        pack_z_kernel,
        out_shape=of((PLACES, Z_ROWS, LANES)),
        compiler_params=params(),
        cost_estimate=cost(0, 2 * 6 * TOK * WIDTH, 0),
        name="pack_z",
    )(q, k, v)
    mine = z_exchange(to_z)
    to_cam = pl.pallas_call(
        pack_cam_kernel,
        out_shape=[of((C_ROWS, LANES))] * CAMS,
        in_specs=[smem] * 2 + [vmem] * 4,
        compiler_params=params(),
        cost_estimate=cost(0, 2 * 8 * TOK * WIDTH, 0),
        name="pack_cam",
    )(bev_list, bev_count, q, bev_keys, bev_values, strip_kv[0])
    got = [to_cam[0]]
    for i in range(1, CAMS):
        x_hi, y = AWAY[i]
        moves = [
            (NY * a + b, NY * ((a + x_hi) % 2) + (b + y) % NY) for a in range(2) for b in range(NY)
        ]
        got.append(lax.ppermute(to_cam[i], "cam", moves))
    mine = after(mine, *got)
    other = lax.ppermute(mine, "seq", [(s, s ^ 1) for s in range(4 * NZ)])
    cam_out = pl.pallas_call(
        cam_kernel,
        out_shape=of((CAMS, CO_ROWS, LANES)),
        scratch_shapes=[
            pltpu.VMEM((CAMS, C_ROWS, LANES), BF),
            pltpu.VMEM((CAMS, LANES), jnp.int32),
            pltpu.SMEM((CAMS, LANES), jnp.int32),
        ],
        compiler_params=params(),
        cost_estimate=cost(4 * 4 * TOK * 448 * WIDTH, 4 * TOK * WIDTH, TOK * 448 * 24),
        name="cam_attention",
    )(*got, gains)
    cam_back = cam_exchange(cam_out)
    self_out = pl.pallas_call(
        self_kernel,
        out_shape=of((PLACES, O_ROWS, LANES)),
        scratch_shapes=[
            pltpu.VMEM((2, KEYS, 2 * LANES), BF),
            pltpu.VMEM((3 * NZ * TOK, LANES), BF),
            pltpu.VMEM((2, BQ, KEYS), F32),
            pltpu.VMEM((2, BQ, LANES), F32),
            pltpu.VMEM((3 * NZ * TOK, LANES), F32),
        ],
        compiler_params=params(),
        cost_estimate=cost(4 * 4 * TOK * KEYS * WIDTH, 4 * KEYS * 384, TOK * KEYS * 24),
        name="self_attention",
    )(mine, other)
    self_back = z_exchange(self_out)
    blended = pl.pallas_call(
        blend_kernel,
        out_shape=of((TOK, WIDTH)),
        compiler_params=params(),
        cost_estimate=cost(0, 10 * TOK * WIDTH, 0),
        name="blend",
    )(self_back, cam_back, gains)
    return blended[None]


def solution(mesh):
    return jax.shard_map(
        shards,
        mesh=mesh,
        in_specs=(
            P("cam", "seq", None),
            P("cam", "seq", None),
            P("cam", "seq", None),
            P("cam", None, None, "seq", None),
            P(("cam", "seq"), None),
            P(("cam", "seq"), None),
            P("cam", "seq", None),
            P("cam", "seq"),
            P(),
            P(),
        ),
        out_specs=P("cam", "seq", None),
        check_vma=False,
    )
```

```python
import functools
import math

import jax
import jax.numpy as jnp
from jax import lax
from jax.experimental import pallas as pl
from jax.experimental.pallas import tpu as pltpu
from jax.sharding import PartitionSpec as P

BF = jnp.bfloat16
F32 = jnp.float32
LANES = 128
HALF = 64
LIST = 3
NZ = 8
CAMS = 8
NY = 4
GROUP_PAIRS = 3
GROUP_COLS = GROUP_PAIRS * 128
PLACES = 2 * NZ
TOK = 128
EDGE = 32
WIDTH = 1536
KEYS = 4096
META = 16
BQ = 256
KT = 256
V_ROWS = 80
SCALE = math.log2(math.e) / math.sqrt(HALF)
NT = (((1,), (1,)), ((), ()))
VMEM_LIMIT = 56 * 2**20

Q_ONE = TOK
KV_TWO = Q_ONE + TOK // 2
Q_TWO = KV_TWO + TOK
Z_ROWS = Q_TWO + TOK // 4
O_ROWS = TOK // 2 + TOK // 4

C_V = TOK
C_Q = 2 * TOK
C_META = 3 * TOK
C_ROWS = C_META + META


def low_lanes(rows):
    return lax.broadcasted_iota(jnp.int32, (rows, LANES), 1) < HALF


def half_turn(x):
    return pltpu.roll(x, HALF, 1)


def side_by_side(a, a_half, b, b_half):
    left = half_turn(a) if a_half else a
    right = b if b_half else half_turn(b)
    return jnp.where(low_lanes(a.shape[0]), left, right)


def folded(x, half):
    n = x.shape[0] // 2
    return side_by_side(x[:n], half, x[n:], half)


def tile(ref, index):
    return ref[:, index * LANES : (index + 1) * LANES]


def params():
    return pltpu.CompilerParams(vmem_limit_bytes=VMEM_LIMIT)


def pack_z_kernel(q_ref, k_ref, v_ref, out_ref):
    for z in range(NZ):
        at, half = NZ + z // 2, z % 2
        shared = side_by_side(tile(k_ref, at), half, tile(v_ref, at), half)
        q_shared = tile(q_ref, at)
        k, v, q = tile(k_ref, z), tile(v_ref, z), tile(q_ref, z)
        for x in range(2):
            place = 2 * z + x
            out_ref[place, :Q_ONE] = side_by_side(k, x, v, x)
            out_ref[place, Q_ONE:KV_TWO] = folded(q, x)
            out_ref[place, KV_TWO:Q_TWO] = shared
            out_ref[place, Q_TWO:] = folded(q_shared[x * HALF : (x + 1) * HALF], half)


def pack_cam_kernel(list_ref, count_ref, q_ref, k_ref, v_ref, *outs):
    y = lax.rem(lax.axis_index("cam"), NY)
    lane = lax.broadcasted_iota(jnp.int32, (META, GROUP_COLS), 1)
    uses = jnp.where(lane == LIST, count_ref[0, 0], 0)
    for j in range(LIST):
        uses = jnp.where(lane == j, list_ref[0, 0, j], uses)
    uses = uses.astype(F32).astype(BF)
    for d, out_ref in enumerate(outs):
        cols = pl.ds(pl.multiple_of(lax.rem(y + d, NY) * GROUP_COLS, LANES), GROUP_COLS)
        out_ref[:C_V] = k_ref[:, cols]
        out_ref[C_V:C_Q] = v_ref[:, cols]
        out_ref[C_Q:C_META] = q_ref[:, cols]
        out_ref[C_META:] = uses


def self_kernel(mine_ref, other_ref, o_ref, v_all, q_all, s_buf, m_buf, o_all):
    both = (mine_ref, other_ref)
    for i, ref in enumerate(both):
        for place in range(PLACES):
            cols = slice((i * PLACES + place) * TOK, (i * PLACES + place + 1) * TOK)
            v_all[0, :HALF, cols] = ref[place, :TOK].T[HALF:]
            v_all[1, :HALF, cols] = ref[place, KV_TWO:Q_TWO].T[HALF:]
    v_all[:, HALF:] = jnp.ones((2, V_ROWS - HALF, KEYS), BF)

    def unfold(q, at):
        n = q.shape[0]
        low, nil = low_lanes(n), jnp.zeros((n, LANES), BF)
        q_all[at : at + n] = jnp.where(low, q, nil)
        q_all[at + n : at + 2 * n] = jnp.where(low, half_turn(q), nil)

    first = PLACES * TOK
    for place in range(PLACES):
        unfold(mine_ref[place, Q_ONE:KV_TWO], place * TOK)
        unfold(mine_ref[place, Q_TWO:], first + place * HALF)
    change = first // BQ
    steps = change + change // 2

    def scores(i, slot):
        rows = pl.ds(pl.multiple_of(i // change * KV_TWO, HALF), TOK)
        q = q_all[pl.ds(pl.multiple_of(i * BQ, BQ), BQ)]
        largest = jnp.full((8, BQ), -jnp.inf, F32)
        for t in range(2 * PLACES):
            keys = both[t // PLACES][t % PLACES, rows]
            s = lax.dot_general(keys, q, NT, preferred_element_type=F32)
            s_buf[slot, t * TOK : (t + 1) * TOK] = s
            largest = jnp.maximum(largest, jnp.max(s.reshape(TOK // 8, 8, BQ), axis=0))
        top = jnp.max(largest, axis=0, keepdims=True) * SCALE
        m_buf[slot] = jnp.broadcast_to(top, (8, BQ))

    def values(i, slot):
        top = m_buf[slot][:1]
        total = jnp.zeros((V_ROWS, BQ), F32)
        for t in range(KEYS // KT):
            s = s_buf[slot, t * KT : (t + 1) * KT]
            w = jnp.exp2(s * SCALE - top).astype(BF)
            total = total + jnp.dot(
                v_all[i // change, :, t * KT : (t + 1) * KT], w, preferred_element_type=F32
            )
        out = total[:HALF] / total[HALF : HALF + 1]
        out = jnp.concatenate([out, out], axis=0).T
        o_all[pl.ds(pl.multiple_of(i * BQ, BQ), BQ)] = out

    scores(0, 0)

    def two_steps(j, carry):
        i = 2 * j
        scores(i + 1, 1)
        values(i, 0)
        scores(jnp.minimum(i + 2, steps - 1), 0)
        values(i + 1, 1)
        return carry

    lax.fori_loop(0, steps // 2, two_steps, 0)

    def fold(at, n):
        return jnp.where(low_lanes(n), o_all[at : at + n], o_all[at + n : at + 2 * n]).astype(BF)

    for place in range(PLACES):
        o_ref[place, : TOK // 2] = fold(place * TOK, TOK // 2)
        o_ref[place, TOK // 2 :] = fold(first + place * HALF, TOK // 4)


def attention(q, blocks, allowed=None):
    scores = [lax.dot_general(q, keys, NT, preferred_element_type=F32) for keys, _ in blocks]
    if allowed is not None:
        scores = [jnp.where(ok, s, -1e30) for ok, s in zip(allowed, scores)]
    top = jnp.max(functools.reduce(jnp.maximum, scores), axis=1, keepdims=True) * SCALE
    weights = jnp.concatenate([jnp.exp2(s * SCALE - top).astype(BF) for s in scores], axis=1)
    wide = jnp.concatenate([v for _, v in blocks], axis=0)
    wide = jnp.concatenate([wide, jnp.ones_like(wide)], axis=1)
    total = jnp.dot(weights, wide, preferred_element_type=F32)
    return total[:, :LANES] / total[:, LANES:]


def pair_attention(q, blocks, allowed=None):
    low, nil = low_lanes(TOK), jnp.zeros_like(q)
    both = jnp.concatenate([jnp.where(low, q, nil), jnp.where(low, nil, q)], axis=0)
    out = attention(both, blocks, allowed)
    return jnp.where(low, out[:TOK], out[TOK:])


def view_kernel(q_ref, left_ref, right_ref, out_ref):
    for i in range(WIDTH // LANES):
        cols = slice(i * LANES, (i + 1) * LANES)
        keys = jnp.concatenate([left_ref[0, :, cols], right_ref[0, :, cols]], axis=0)
        vals = jnp.concatenate([left_ref[1, :, cols], right_ref[1, :, cols]], axis=0)
        out_ref[:, cols] = pair_attention(q_ref[:, cols], [(keys, vals)])


def layout_kernel(*refs):
    in_refs, far_ref, o_refs = refs[:NY], refs[NY], refs[NY + 1 : 2 * NY + 1]
    kv_all, uses_vec, uses_ref = refs[2 * NY + 1 :]
    cam = lax.axis_index("cam")
    x_hi, y = cam // NY, lax.rem(cam, NY)
    for d in range(NY):
        uses_vec[d : d + 1] = in_refs[d][C_META:, :LANES].astype(F32)[:1].astype(jnp.int32)
    uses_vec[NY:] = jnp.zeros((NY, LANES), jnp.int32)
    pltpu.sync_copy(uses_vec, uses_ref)
    for d in range(NY):
        kv_all[d] = in_refs[d][:C_Q]
        kv_all[NY + d] = far_ref[d * C_Q : (d + 1) * C_Q]
    for d in range(NY):
        places, allowed = [], []
        for j in range(LIST):
            e = uses_ref[d, j]
            place = lax.rem(y - lax.rem(e, NY) + NY, NY)
            places.append(jnp.where(e // NY == x_hi, place, place + NY))
            allowed.append(j < uses_ref[d, LIST])
        for p in range(GROUP_PAIRS):
            cols = slice(p * LANES, (p + 1) * LANES)
            blocks = [(kv_all[e, :C_V, cols], kv_all[e, C_V:, cols]) for e in places]
            q = in_refs[d][C_Q:C_META, cols]
            o_refs[d][:, cols] = pair_attention(q, blocks, allowed).astype(BF)


def blend_kernel(self_ref, *refs):
    cam_refs = refs[:NY]
    view_ref, gain_ref, out_ref, cam_all = refs[NY:]
    y = lax.rem(lax.axis_index("cam"), NY)
    for d in range(NY):
        cam_all[lax.rem(y + d, NY)] = cam_refs[d][...]

    def unfolded(x, y, n):
        lower = side_by_side(x, 0, y, 0)
        upper = side_by_side(x, 1, y, 1)
        return jnp.concatenate([lower, upper], axis=0)

    for i in range(WIDTH // LANES):
        cols = slice(i * LANES, (i + 1) * LANES)
        if i < NZ:
            one, two = (self_ref[2 * i + x, : TOK // 2].astype(F32) for x in range(2))
            mine = unfolded(one, two, HALF)
        else:
            z = 2 * (i - NZ)
            parts = []
            for x in range(2):
                one, two = (self_ref[2 * (z + k) + x, TOK // 2 :].astype(F32) for k in range(2))
                parts.append(unfolded(one, two, HALF // 2))
            mine = jnp.concatenate(parts, axis=0)
        at = i % GROUP_PAIRS
        other = cam_all[i // GROUP_PAIRS, :, at * LANES : (at + 1) * LANES].astype(F32)
        blended = gain_ref[0:1, cols] * mine + gain_ref[1:2, cols] * view_ref[:, cols]
        out_ref[:, cols] = (blended + gain_ref[2:3, cols] * other).astype(BF)


def of(shape, dtype=BF):
    return jax.ShapeDtypeStruct(shape, dtype)


def cost(flops, moved, exps):
    return pl.CostEstimate(flops=flops, bytes_accessed=moved, transcendentals=exps)


def after(x, *done):
    return lax.optimization_barrier((x,) + done)[0]


SAME_CORE = [[4 * z + 2 * x + c for z in range(NZ) for x in range(2)] for c in range(2)]


def z_exchange(x):
    return lax.all_to_all(x, "seq", 0, 0, axis_index_groups=SAME_CORE, tiled=True)


def y_send(x, by):
    moves = [(NY * a + b, NY * a + (b + by) % NY) for a in range(2) for b in range(NY)]
    return lax.ppermute(x, "cam", moves)


def shards(
    q_tok, k_tok, v_tok, strip_kv, bev_keys, bev_values, bev_list, bev_count, gate_table, timestep
):
    q, k, v = q_tok[0], k_tok[0], v_tok[0]
    smem = pl.BlockSpec(memory_space=pltpu.SMEM)
    vmem = pl.BlockSpec(memory_space=pltpu.VMEM)
    gains = lax.dynamic_index_in_dim(gate_table, timestep[0], 0, keepdims=False)
    to_z = pl.pallas_call(
        pack_z_kernel,
        out_shape=of((PLACES, Z_ROWS, LANES)),
        compiler_params=params(),
        cost_estimate=cost(0, 2 * 6 * TOK * WIDTH, 0),
        name="pack_z",
    )(q, k, v)
    mine = z_exchange(to_z)
    to_cam = pl.pallas_call(
        pack_cam_kernel,
        out_shape=[of((C_ROWS, GROUP_COLS))] * NY,
        in_specs=[smem] * 2 + [vmem] * 3,
        compiler_params=params(),
        cost_estimate=cost(0, 2 * 6 * TOK * WIDTH, 0),
        name="pack_cam",
    )(bev_list, bev_count, q, bev_keys, bev_values)
    got = [to_cam[0]] + [y_send(to_cam[d], d) for d in range(1, NY)]
    ring = range(CAMS)
    from_left = lax.ppermute(strip_kv[0, 1], "cam", [(c, (c + 1) % CAMS) for c in ring])
    from_right = lax.ppermute(strip_kv[0, 0], "cam", [(c, (c - 1) % CAMS) for c in ring])
    view = pl.pallas_call(
        view_kernel,
        out_shape=of((TOK, WIDTH), F32),
        compiler_params=params(),
        cost_estimate=cost(16 * TOK * 64 * WIDTH, 4 * TOK * WIDTH, TOK * 64 * 24),
        name="view_attention",
    )(q, from_left, from_right)
    to_far = jnp.concatenate([t[:C_Q] for t in got], axis=0)
    far = lax.ppermute(to_far, "cam", [(c, (c + NY) % CAMS) for c in ring])
    mine = after(mine, view, to_far)
    other = lax.ppermute(mine, "seq", [(s, s ^ 1) for s in range(4 * NZ)])
    queries = 3 * NZ * TOK
    self_out = pl.pallas_call(
        self_kernel,
        out_shape=of((PLACES, O_ROWS, LANES)),
        scratch_shapes=[
            pltpu.VMEM((2, V_ROWS, KEYS), BF),
            pltpu.VMEM((queries, LANES), BF),
            pltpu.VMEM((2, KEYS, BQ), F32),
            pltpu.VMEM((2, 8, BQ), F32),
            pltpu.VMEM((queries, LANES), F32),
        ],
        compiler_params=params(),
        cost_estimate=cost(16 * queries * KEYS * HALF, 8 * KEYS * LANES, queries * KEYS),
        name="self_attention",
    )(mine, other)
    self_back = z_exchange(self_out)
    far = after(far, self_out)
    layout_out = pl.pallas_call(
        layout_kernel,
        out_shape=[of((TOK, GROUP_COLS))] * NY,
        scratch_shapes=[
            pltpu.VMEM((CAMS, C_Q, GROUP_COLS), BF),
            pltpu.VMEM((CAMS, LANES), jnp.int32),
            pltpu.SMEM((CAMS, LANES), jnp.int32),
        ],
        compiler_params=params(),
        cost_estimate=cost(16 * TOK * 384 * WIDTH, 4 * TOK * WIDTH, TOK * 384 * 24),
        name="layout_attention",
    )(*got, far)
    cam_back = [layout_out[0]] + [y_send(layout_out[d], NY - d) for d in range(1, NY)]
    blended = pl.pallas_call(
        blend_kernel,
        out_shape=of((TOK, WIDTH)),
        scratch_shapes=[pltpu.VMEM((NY, TOK, GROUP_COLS), BF)],
        compiler_params=params(),
        cost_estimate=cost(0, 10 * TOK * WIDTH, 0),
        name="blend",
    )(self_back, *cam_back, view, gains)
    return blended[None]


def solution(mesh):
    return jax.shard_map(
        shards,
        mesh=mesh,
        in_specs=(
            P("cam", "seq", None),
            P("cam", "seq", None),
            P("cam", "seq", None),
            P("cam", None, None, "seq", None),
            P(("cam", "seq"), None),
            P(("cam", "seq"), None),
            P("cam", "seq", None),
            P("cam", "seq"),
            P(),
            P(),
        ),
        out_specs=P("cam", "seq", None),
        check_vma=False,
    )
```

```python
import functools
import math

import jax
import jax.numpy as jnp
from jax import lax
from jax.experimental import pallas as pl
from jax.experimental.pallas import tpu as pltpu
from jax.sharding import PartitionSpec as P

BF = jnp.bfloat16
F32 = jnp.float32
LANES = 128
HALF = 64
LIST = 3
NZ = 8
CAMS = 8
NY = 4
GROUP_PAIRS = 3
GROUP_COLS = GROUP_PAIRS * 128
PLACES = 2 * NZ
TOK = 128
EDGE = 32
WIDTH = 1536
KEYS = 4096
META = 16
BQ = 256
KT = 256
V_ROWS = 80
SCALE = math.log2(math.e) / math.sqrt(HALF)
NT = (((1,), (1,)), ((), ()))
MIB = 2**20

Q_ONE = TOK
KV_TWO = Q_ONE + TOK // 2
Q_TWO = KV_TWO + TOK
Z_ROWS = Q_TWO + TOK // 4
O_ROWS = TOK // 2 + TOK // 4

C_V = TOK
C_Q = 2 * TOK
C_META = 3 * TOK
C_ROWS = C_META + META


def low_lanes(rows):
    return lax.broadcasted_iota(jnp.int32, (rows, LANES), 1) < HALF


def half_turn(x):
    return pltpu.roll(x, HALF, 1)


def side_by_side(a, a_half, b, b_half):
    left = half_turn(a) if a_half else a
    right = b if b_half else half_turn(b)
    return jnp.where(low_lanes(a.shape[0]), left, right)


def folded(x, half):
    n = x.shape[0] // 2
    return side_by_side(x[:n], half, x[n:], half)


def tile(ref, index):
    return ref[:, index * LANES : (index + 1) * LANES]


def params(mib=12):
    return pltpu.CompilerParams(vmem_limit_bytes=mib * MIB)


def pack_z_kernel(q_hbm, k_hbm, v_hbm, out_ref, q_ref, k_ref, v_ref, sems):
    pairs = ((k_hbm, k_ref), (v_hbm, v_ref), (q_hbm, q_ref))
    copies = [pltpu.make_async_copy(a, b, sems.at[i]) for i, (a, b) in enumerate(pairs)]
    for copy in copies:
        copy.start()
    for copy in copies:
        copy.wait()
    for z in range(NZ):
        at, half = NZ + z // 2, z % 2
        shared = side_by_side(tile(k_ref, at), half, tile(v_ref, at), half)
        q_shared = tile(q_ref, at)
        k, v, q = tile(k_ref, z), tile(v_ref, z), tile(q_ref, z)
        for x in range(2):
            place = 2 * z + x
            out_ref[place, :Q_ONE] = side_by_side(k, x, v, x)
            out_ref[place, Q_ONE:KV_TWO] = folded(q, x)
            out_ref[place, KV_TWO:Q_TWO] = shared
            out_ref[place, Q_TWO:] = folded(q_shared[x * HALF : (x + 1) * HALF], half)


def pack_cam_kernel(list_ref, count_ref, q_ref, k_ref, v_ref, *outs):
    y = lax.rem(lax.axis_index("cam"), NY)
    lane = lax.broadcasted_iota(jnp.int32, (META, GROUP_COLS), 1)
    uses = jnp.where(lane == LIST, count_ref[0, 0], 0)
    for j in range(LIST):
        uses = jnp.where(lane == j, list_ref[0, 0, j], uses)
    uses = uses.astype(F32).astype(BF)
    for d, out_ref in enumerate(outs):
        cols = pl.ds(pl.multiple_of(lax.rem(y + d, NY) * GROUP_COLS, LANES), GROUP_COLS)
        out_ref[:C_V] = k_ref[:, cols]
        out_ref[C_V:C_Q] = v_ref[:, cols]
        out_ref[C_Q:C_META] = q_ref[:, cols]
        out_ref[C_META:] = uses


def self_kernel(mine_ref, other_ref, o_ref, v_all, q_all, s_buf, m_buf, o_all):
    both = (mine_ref, other_ref)
    for i, ref in enumerate(both):
        for place in range(PLACES):
            cols = slice((i * PLACES + place) * TOK, (i * PLACES + place + 1) * TOK)
            v_all[0, :HALF, cols] = ref[place, :TOK].T[HALF:]
            v_all[1, :HALF, cols] = ref[place, KV_TWO:Q_TWO].T[HALF:]
    v_all[:, HALF:] = jnp.ones((2, V_ROWS - HALF, KEYS), BF)

    def unfold(q, at):
        n = q.shape[0]
        low, nil = low_lanes(n), jnp.zeros((n, LANES), BF)
        q_all[at : at + n] = jnp.where(low, q, nil)
        q_all[at + n : at + 2 * n] = jnp.where(low, half_turn(q), nil)

    first = PLACES * TOK
    for place in range(PLACES):
        unfold(mine_ref[place, Q_ONE:KV_TWO], place * TOK)
        unfold(mine_ref[place, Q_TWO:], first + place * HALF)
    change = first // BQ
    steps = change + change // 2

    def scores(i, slot):
        rows = pl.ds(pl.multiple_of(i // change * KV_TWO, HALF), TOK)
        q = q_all[pl.ds(pl.multiple_of(i * BQ, BQ), BQ)]
        largest = jnp.full((8, BQ), -jnp.inf, F32)
        for t in range(2 * PLACES):
            keys = both[t // PLACES][t % PLACES, rows]
            s = lax.dot_general(keys, q, NT, preferred_element_type=F32)
            s_buf[slot, t * TOK : (t + 1) * TOK] = s
            largest = jnp.maximum(largest, jnp.max(s.reshape(TOK // 8, 8, BQ), axis=0))
        top = jnp.max(largest, axis=0, keepdims=True) * SCALE
        m_buf[slot] = jnp.broadcast_to(top, (8, BQ))

    def values(i, slot):
        top = m_buf[slot][:1]
        total = jnp.zeros((V_ROWS, BQ), F32)
        for t in range(KEYS // KT):
            s = s_buf[slot, t * KT : (t + 1) * KT]
            w = jnp.exp2(s * SCALE - top).astype(BF)
            total = total + jnp.dot(
                v_all[i // change, :, t * KT : (t + 1) * KT], w, preferred_element_type=F32
            )
        out = total[:HALF] / total[HALF : HALF + 1]
        out = jnp.concatenate([out, out], axis=0).T
        o_all[pl.ds(pl.multiple_of(i * BQ, BQ), BQ)] = out

    scores(0, 0)

    def two_steps(j, carry):
        i = 2 * j
        scores(i + 1, 1)
        values(i, 0)
        scores(jnp.minimum(i + 2, steps - 1), 0)
        values(i + 1, 1)
        return carry

    lax.fori_loop(0, steps // 2, two_steps, 0)

    def fold(at, n):
        return jnp.where(low_lanes(n), o_all[at : at + n], o_all[at + n : at + 2 * n]).astype(BF)

    for place in range(PLACES):
        o_ref[place, : TOK // 2] = fold(place * TOK, TOK // 2)
        o_ref[place, TOK // 2 :] = fold(first + place * HALF, TOK // 4)


def attention(q, blocks, allowed=None):
    scores = [lax.dot_general(q, keys, NT, preferred_element_type=F32) for keys, _ in blocks]
    if allowed is not None:
        scores = [jnp.where(ok, s, -1e30) for ok, s in zip(allowed, scores)]
    top = jnp.max(functools.reduce(jnp.maximum, scores), axis=1, keepdims=True) * SCALE
    weights = jnp.concatenate([jnp.exp2(s * SCALE - top).astype(BF) for s in scores], axis=1)
    wide = jnp.concatenate([v for _, v in blocks], axis=0)
    wide = jnp.concatenate([wide, jnp.ones_like(wide)], axis=1)
    total = jnp.dot(weights, wide, preferred_element_type=F32)
    return total[:, :LANES] / total[:, LANES:]


def pair_attention(q, blocks, allowed=None):
    low, nil = low_lanes(TOK), jnp.zeros_like(q)
    both = jnp.concatenate([jnp.where(low, q, nil), jnp.where(low, nil, q)], axis=0)
    out = attention(both, blocks, allowed)
    return jnp.where(low, out[:TOK], out[TOK:])


def view_kernel(q_ref, left_ref, right_ref, out_ref):
    for i in range(WIDTH // LANES):
        cols = slice(i * LANES, (i + 1) * LANES)
        keys = jnp.concatenate([left_ref[0, :, cols], right_ref[0, :, cols]], axis=0)
        vals = jnp.concatenate([left_ref[1, :, cols], right_ref[1, :, cols]], axis=0)
        out_ref[:, cols] = pair_attention(q_ref[:, cols], [(keys, vals)])


def layout_kernel(*refs):
    in_refs, far_ref, o_refs = refs[:NY], refs[NY], refs[NY + 1 : 2 * NY + 1]
    kv_all, uses_vec, uses_ref = refs[2 * NY + 1 :]
    cam = lax.axis_index("cam")
    x_hi, y = cam // NY, lax.rem(cam, NY)
    for d in range(NY):
        uses_vec[d : d + 1] = in_refs[d][C_META:, :LANES].astype(F32)[:1].astype(jnp.int32)
    uses_vec[NY:] = jnp.zeros((NY, LANES), jnp.int32)
    pltpu.sync_copy(uses_vec, uses_ref)
    for d in range(NY):
        kv_all[d] = in_refs[d][:C_Q]
        kv_all[NY + d] = far_ref[d * C_Q : (d + 1) * C_Q]
    for d in range(NY):
        places, allowed = [], []
        for j in range(LIST):
            e = uses_ref[d, j]
            place = lax.rem(y - lax.rem(e, NY) + NY, NY)
            places.append(jnp.where(e // NY == x_hi, place, place + NY))
            allowed.append(j < uses_ref[d, LIST])
        for p in range(GROUP_PAIRS):
            cols = slice(p * LANES, (p + 1) * LANES)
            blocks = [(kv_all[e, :C_V, cols], kv_all[e, C_V:, cols]) for e in places]
            q = in_refs[d][C_Q:C_META, cols]
            o_refs[d][:, cols] = pair_attention(q, blocks, allowed).astype(BF)


def blend_kernel(self_ref, *refs):
    cam_refs = refs[:NY]
    view_ref, gain_ref, out_ref, cam_all = refs[NY:]
    y = lax.rem(lax.axis_index("cam"), NY)
    for d in range(NY):
        cam_all[lax.rem(y + d, NY)] = cam_refs[d][...]

    def unfolded(x, y, n):
        lower = side_by_side(x, 0, y, 0)
        upper = side_by_side(x, 1, y, 1)
        return jnp.concatenate([lower, upper], axis=0)

    for i in range(WIDTH // LANES):
        cols = slice(i * LANES, (i + 1) * LANES)
        if i < NZ:
            one, two = (self_ref[2 * i + x, : TOK // 2].astype(F32) for x in range(2))
            mine = unfolded(one, two, HALF)
        else:
            z = 2 * (i - NZ)
            parts = []
            for x in range(2):
                one, two = (self_ref[2 * (z + k) + x, TOK // 2 :].astype(F32) for k in range(2))
                parts.append(unfolded(one, two, HALF // 2))
            mine = jnp.concatenate(parts, axis=0)
        at = i % GROUP_PAIRS
        other = cam_all[i // GROUP_PAIRS, :, at * LANES : (at + 1) * LANES].astype(F32)
        blended = gain_ref[0:1, cols] * mine + gain_ref[1:2, cols] * view_ref[:, cols]
        out_ref[:, cols] = (blended + gain_ref[2:3, cols] * other).astype(BF)


def of(shape, dtype=BF):
    return jax.ShapeDtypeStruct(shape, dtype)


def cost(flops, moved, exps):
    return pl.CostEstimate(flops=flops, bytes_accessed=moved, transcendentals=exps)


def after(x, *done):
    return lax.optimization_barrier((x,) + done)[0]


SAME_CORE = [[4 * z + 2 * x + c for z in range(NZ) for x in range(2)] for c in range(2)]


def z_exchange(x):
    return lax.all_to_all(x, "seq", 0, 0, axis_index_groups=SAME_CORE, tiled=True)


def y_send(x, by):
    moves = [(NY * a + b, NY * a + (b + by) % NY) for a in range(2) for b in range(NY)]
    return lax.ppermute(x, "cam", moves)


def shards(
    q_tok, k_tok, v_tok, strip_kv, bev_keys, bev_values, bev_list, bev_count, gate_table, timestep
):
    q, k, v = q_tok[0], k_tok[0], v_tok[0]
    smem = pl.BlockSpec(memory_space=pltpu.SMEM)
    vmem = pl.BlockSpec(memory_space=pltpu.VMEM)
    gains = lax.dynamic_index_in_dim(gate_table, timestep[0], 0, keepdims=False)
    to_z = pl.pallas_call(
        pack_z_kernel,
        out_shape=of((PLACES, Z_ROWS, LANES)),
        in_specs=[pl.BlockSpec(memory_space=pltpu.HBM)] * 3,
        scratch_shapes=[pltpu.VMEM((TOK, WIDTH), BF)] * 3 + [pltpu.SemaphoreType.DMA((3,))],
        compiler_params=params(),
        cost_estimate=cost(0, 2 * 6 * TOK * WIDTH, 0),
        name="pack_z",
    )(*(pltpu.with_memory_space_constraint(t, pltpu.HBM) for t in (q, k, v)))
    mine = z_exchange(to_z)
    to_cam = pl.pallas_call(
        pack_cam_kernel,
        out_shape=[of((C_ROWS, GROUP_COLS))] * NY,
        in_specs=[smem] * 2 + [vmem] * 3,
        compiler_params=params(),
        cost_estimate=cost(0, 2 * 6 * TOK * WIDTH, 0),
        name="pack_cam",
    )(bev_list, bev_count, q, bev_keys, bev_values)
    got = [to_cam[0]] + [y_send(to_cam[d], d) for d in range(1, NY)]
    ring = range(CAMS)
    from_left = lax.ppermute(strip_kv[0, 1], "cam", [(c, (c + 1) % CAMS) for c in ring])
    from_right = lax.ppermute(strip_kv[0, 0], "cam", [(c, (c - 1) % CAMS) for c in ring])
    view = pl.pallas_call(
        view_kernel,
        out_shape=of((TOK, WIDTH), F32),
        compiler_params=params(),
        cost_estimate=cost(16 * TOK * 64 * WIDTH, 4 * TOK * WIDTH, TOK * 64 * 24),
        name="view_attention",
    )(q, from_left, from_right)
    to_far = jnp.concatenate([t[:C_Q] for t in got], axis=0)
    far = lax.ppermute(to_far, "cam", [(c, (c + NY) % CAMS) for c in ring])
    mine = after(mine, view, to_far, gains)
    other = lax.ppermute(mine, "seq", [(s, s ^ 1) for s in range(4 * NZ)])
    queries = 3 * NZ * TOK
    self_out = pl.pallas_call(
        self_kernel,
        out_shape=of((PLACES, O_ROWS, LANES)),
        scratch_shapes=[
            pltpu.VMEM((2, V_ROWS, KEYS), BF),
            pltpu.VMEM((queries, LANES), BF),
            pltpu.VMEM((2, KEYS, BQ), F32),
            pltpu.VMEM((2, 8, BQ), F32),
            pltpu.VMEM((queries, LANES), F32),
        ],
        compiler_params=params(24),
        cost_estimate=cost(16 * queries * KEYS * HALF, 8 * KEYS * LANES, queries * KEYS),
        name="self_attention",
    )(mine, other)
    self_back = z_exchange(self_out)
    far = after(far, self_out)
    layout_out = pl.pallas_call(
        layout_kernel,
        out_shape=[of((TOK, GROUP_COLS))] * NY,
        scratch_shapes=[
            pltpu.VMEM((CAMS, C_Q, GROUP_COLS), BF),
            pltpu.VMEM((CAMS, LANES), jnp.int32),
            pltpu.SMEM((CAMS, LANES), jnp.int32),
        ],
        compiler_params=params(),
        cost_estimate=cost(16 * TOK * 384 * WIDTH, 4 * TOK * WIDTH, TOK * 384 * 24),
        name="layout_attention",
    )(*got, far)
    cam_back = [layout_out[0]] + [y_send(layout_out[d], NY - d) for d in range(1, NY)]
    blended = pl.pallas_call(
        blend_kernel,
        out_shape=of((TOK, WIDTH)),
        scratch_shapes=[pltpu.VMEM((NY, TOK, GROUP_COLS), BF)],
        compiler_params=params(),
        cost_estimate=cost(0, 10 * TOK * WIDTH, 0),
        name="blend",
    )(self_back, *cam_back, view, gains)
    return blended[None]


def solution(mesh):
    return jax.shard_map(
        shards,
        mesh=mesh,
        in_specs=(
            P("cam", "seq", None),
            P("cam", "seq", None),
            P("cam", "seq", None),
            P("cam", None, None, "seq", None),
            P(("cam", "seq"), None),
            P(("cam", "seq"), None),
            P("cam", "seq", None),
            P("cam", "seq"),
            P(),
            P(),
        ),
        out_specs=P("cam", "seq", None),
        check_vma=False,
    )
```

```python
import functools
import math

import jax
import jax.numpy as jnp
from jax import lax
from jax.experimental import pallas as pl
from jax.experimental.pallas import tpu as pltpu
from jax.sharding import PartitionSpec as P

BF = jnp.bfloat16
F32 = jnp.float32
LANES = 128
HALF = 64
LIST = 3
NZ = 8
CAMS = 8
NY = 4
GROUP_PAIRS = 3
GROUP_COLS = GROUP_PAIRS * 128
PLACES = 2 * NZ
TOK = 128
EDGE = 32
WIDTH = 1536
KEYS = 4096
META = 16
BQ = 256
KT = 256
V_ROWS = 80
SCALE = math.log2(math.e) / math.sqrt(HALF)
NT = (((1,), (1,)), ((), ()))
MIB = 2**20

Q_ONE = TOK
KV_TWO = Q_ONE + TOK // 2
Q_TWO = KV_TWO + TOK
Z_ROWS = Q_TWO + TOK // 4
O_ROWS = TOK // 2 + TOK // 4

C_V = TOK
C_Q = 2 * TOK
C_META = 3 * TOK
C_ROWS = C_META + META


def low_lanes(rows):
    return lax.broadcasted_iota(jnp.int32, (rows, LANES), 1) < HALF


def half_turn(x):
    return pltpu.roll(x, HALF, 1)


def side_by_side(a, a_half, b, b_half):
    left = half_turn(a) if a_half else a
    right = b if b_half else half_turn(b)
    return jnp.where(low_lanes(a.shape[0]), left, right)


def folded(x, half):
    n = x.shape[0] // 2
    return side_by_side(x[:n], half, x[n:], half)


def tile(ref, index):
    return ref[:, index * LANES : (index + 1) * LANES]


def params(mib=12):
    return pltpu.CompilerParams(vmem_limit_bytes=mib * MIB)


def pack_z_kernel(q_hbm, k_hbm, v_hbm, out_ref, q_ref, k_ref, v_ref, sems):
    pairs = ((k_hbm, k_ref), (v_hbm, v_ref), (q_hbm, q_ref))
    copies = [pltpu.make_async_copy(a, b, sems.at[i]) for i, (a, b) in enumerate(pairs)]
    for copy in copies:
        copy.start()
    for copy in copies:
        copy.wait()
    for z in range(NZ):
        at, half = NZ + z // 2, z % 2
        shared = side_by_side(tile(k_ref, at), half, tile(v_ref, at), half)
        q_shared = tile(q_ref, at)
        k, v, q = tile(k_ref, z), tile(v_ref, z), tile(q_ref, z)
        for x in range(2):
            place = 2 * z + x
            out_ref[place, :Q_ONE] = side_by_side(k, x, v, x)
            out_ref[place, Q_ONE:KV_TWO] = folded(q, x)
            out_ref[place, KV_TWO:Q_TWO] = shared
            out_ref[place, Q_TWO:] = folded(q_shared[x * HALF : (x + 1) * HALF], half)


def pack_cam_kernel(list_ref, count_ref, q_ref, k_ref, v_ref, *outs):
    y = lax.rem(lax.axis_index("cam"), NY)
    lane = lax.broadcasted_iota(jnp.int32, (META, GROUP_COLS), 1)
    uses = jnp.where(lane == LIST, count_ref[0, 0], 0)
    for j in range(LIST):
        uses = jnp.where(lane == j, list_ref[0, 0, j], uses)
    uses = uses.astype(F32).astype(BF)
    for d, out_ref in enumerate(outs):
        cols = pl.ds(pl.multiple_of(lax.rem(y + d, NY) * GROUP_COLS, LANES), GROUP_COLS)
        out_ref[:C_V] = k_ref[:, cols]
        out_ref[C_V:C_Q] = v_ref[:, cols]
        out_ref[C_Q:C_META] = q_ref[:, cols]
        out_ref[C_META:] = uses


def lay_values(ref, v_all):
    for place in range(PLACES):
        cols = slice(place * TOK, (place + 1) * TOK)
        v_all[0, :HALF, cols] = ref[place, :TOK].T[HALF:]
        v_all[1, :HALF, cols] = ref[place, KV_TWO:Q_TWO].T[HALF:]
    v_all[:, HALF:] = jnp.ones((2, V_ROWS - HALF, KEYS // 2), BF)


def lay_mine_kernel(mine_ref, v_all, q_all):
    lay_values(mine_ref, v_all)

    def unfold(q, at):
        n = q.shape[0]
        low, nil = low_lanes(n), jnp.zeros((n, LANES), BF)
        q_all[at : at + n] = jnp.where(low, q, nil)
        q_all[at + n : at + 2 * n] = jnp.where(low, half_turn(q), nil)

    for place in range(PLACES):
        unfold(mine_ref[place, Q_ONE:KV_TWO], place * TOK)
        unfold(mine_ref[place, Q_TWO:], PLACES * TOK + place * HALF)


def self_kernel(mine_ref, other_ref, v_mine, q_all, o_ref, v_other, s_buf, m_buf, o_all):
    both, v_both = (mine_ref, other_ref), (v_mine, v_other)
    lay_values(other_ref, v_other)
    first = PLACES * TOK
    change = first // BQ
    steps = change + change // 2

    def scores(i, slot):
        rows = pl.ds(pl.multiple_of(i // change * KV_TWO, HALF), TOK)
        q = q_all[pl.ds(pl.multiple_of(i * BQ, BQ), BQ)]
        largest = jnp.full((8, BQ), -jnp.inf, F32)
        for t in range(2 * PLACES):
            keys = both[t // PLACES][t % PLACES, rows]
            s = lax.dot_general(keys, q, NT, preferred_element_type=F32)
            s_buf[slot, t * TOK : (t + 1) * TOK] = s
            largest = jnp.maximum(largest, jnp.max(s.reshape(TOK // 8, 8, BQ), axis=0))
        top = jnp.max(largest, axis=0, keepdims=True) * SCALE
        m_buf[slot] = jnp.broadcast_to(top, (8, BQ))

    def values(i, slot):
        top = m_buf[slot][:1]
        total = jnp.zeros((V_ROWS, BQ), F32)
        for t in range(KEYS // KT):
            s = s_buf[slot, t * KT : (t + 1) * KT]
            w = jnp.exp2(s * SCALE - top).astype(BF)
            half, at = divmod(t * KT, KEYS // 2)
            vals = v_both[half][i // change, :, at : at + KT]
            total = total + jnp.dot(vals, w, preferred_element_type=F32)
        out = total[:HALF] / total[HALF : HALF + 1]
        out = jnp.concatenate([out, out], axis=0).T
        o_all[pl.ds(pl.multiple_of(i * BQ, BQ), BQ)] = out

    scores(0, 0)

    def two_steps(j, carry):
        i = 2 * j
        scores(i + 1, 1)
        values(i, 0)
        scores(jnp.minimum(i + 2, steps - 1), 0)
        values(i + 1, 1)
        return carry

    lax.fori_loop(0, steps // 2, two_steps, 0)

    def fold(at, n):
        return jnp.where(low_lanes(n), o_all[at : at + n], o_all[at + n : at + 2 * n]).astype(BF)

    for place in range(PLACES):
        o_ref[place, : TOK // 2] = fold(place * TOK, TOK // 2)
        o_ref[place, TOK // 2 :] = fold(first + place * HALF, TOK // 4)


def attention(q, blocks, allowed=None):
    scores = [lax.dot_general(q, keys, NT, preferred_element_type=F32) for keys, _ in blocks]
    if allowed is not None:
        scores = [jnp.where(ok, s, -1e30) for ok, s in zip(allowed, scores)]
    top = jnp.max(functools.reduce(jnp.maximum, scores), axis=1, keepdims=True) * SCALE
    weights = jnp.concatenate([jnp.exp2(s * SCALE - top).astype(BF) for s in scores], axis=1)
    wide = jnp.concatenate([v for _, v in blocks], axis=0)
    wide = jnp.concatenate([wide, jnp.ones_like(wide)], axis=1)
    total = jnp.dot(weights, wide, preferred_element_type=F32)
    return total[:, :LANES] / total[:, LANES:]


def pair_attention(q, blocks, allowed=None):
    low, nil = low_lanes(TOK), jnp.zeros_like(q)
    both = jnp.concatenate([jnp.where(low, q, nil), jnp.where(low, nil, q)], axis=0)
    out = attention(both, blocks, allowed)
    return jnp.where(low, out[:TOK], out[TOK:])


def view_kernel(q_ref, left_ref, right_ref, out_ref):
    for i in range(WIDTH // LANES):
        cols = slice(i * LANES, (i + 1) * LANES)
        keys = jnp.concatenate([left_ref[0, :, cols], right_ref[0, :, cols]], axis=0)
        vals = jnp.concatenate([left_ref[1, :, cols], right_ref[1, :, cols]], axis=0)
        out_ref[:, cols] = pair_attention(q_ref[:, cols], [(keys, vals)])


def layout_kernel(*refs):
    in_refs, far_ref, o_refs = refs[:NY], refs[NY], refs[NY + 1 : 2 * NY + 1]
    kv_all, uses_vec, uses_ref, sem = refs[2 * NY + 1 :]
    cam = lax.axis_index("cam")
    x_hi, y = cam // NY, lax.rem(cam, NY)
    for d in range(NY):
        uses_vec[d : d + 1] = in_refs[d][C_META:, :LANES].astype(F32)[:1].astype(jnp.int32)
    uses_vec[NY:] = jnp.zeros((NY, LANES), jnp.int32)
    copy = pltpu.make_async_copy(uses_vec, uses_ref, sem)
    copy.start()
    for d in range(NY):
        kv_all[d] = in_refs[d][:C_Q]
        kv_all[NY + d] = far_ref[d * C_Q : (d + 1) * C_Q]
    copy.wait()
    for d in range(NY):
        places, allowed = [], []
        for j in range(LIST):
            e = uses_ref[d, j]
            place = lax.rem(y - lax.rem(e, NY) + NY, NY)
            places.append(jnp.where(e // NY == x_hi, place, place + NY))
            allowed.append(j < uses_ref[d, LIST])
        for p in range(GROUP_PAIRS):
            cols = slice(p * LANES, (p + 1) * LANES)
            blocks = [(kv_all[e, :C_V, cols], kv_all[e, C_V:, cols]) for e in places]
            q = in_refs[d][C_Q:C_META, cols]
            o_refs[d][:, cols] = pair_attention(q, blocks, allowed).astype(BF)


def blend_kernel(self_ref, *refs):
    cam_refs = refs[:NY]
    view_ref, gain_ref, out_ref, cam_all = refs[NY:]
    y = lax.rem(lax.axis_index("cam"), NY)
    for d in range(NY):
        cam_all[lax.rem(y + d, NY)] = cam_refs[d][...]

    def unfolded(x, y, n):
        lower = side_by_side(x, 0, y, 0)
        upper = side_by_side(x, 1, y, 1)
        return jnp.concatenate([lower, upper], axis=0)

    for i in range(WIDTH // LANES):
        cols = slice(i * LANES, (i + 1) * LANES)
        if i < NZ:
            one, two = (self_ref[2 * i + x, : TOK // 2].astype(F32) for x in range(2))
            mine = unfolded(one, two, HALF)
        else:
            z = 2 * (i - NZ)
            parts = []
            for x in range(2):
                one, two = (self_ref[2 * (z + k) + x, TOK // 2 :].astype(F32) for k in range(2))
                parts.append(unfolded(one, two, HALF // 2))
            mine = jnp.concatenate(parts, axis=0)
        at = i % GROUP_PAIRS
        other = cam_all[i // GROUP_PAIRS, :, at * LANES : (at + 1) * LANES].astype(F32)
        blended = gain_ref[0:1, cols] * mine + gain_ref[1:2, cols] * view_ref[:, cols]
        out_ref[:, cols] = (blended + gain_ref[2:3, cols] * other).astype(BF)


def of(shape, dtype=BF):
    return jax.ShapeDtypeStruct(shape, dtype)


def cost(flops, moved, exps):
    return pl.CostEstimate(flops=flops, bytes_accessed=moved, transcendentals=exps)


def after(x, *done):
    return lax.optimization_barrier((x,) + done)[0]


SAME_CORE = [[4 * z + 2 * x + c for z in range(NZ) for x in range(2)] for c in range(2)]


def z_exchange(x):
    return lax.all_to_all(x, "seq", 0, 0, axis_index_groups=SAME_CORE, tiled=True)


def y_send(x, by):
    moves = [(NY * a + b, NY * a + (b + by) % NY) for a in range(2) for b in range(NY)]
    return lax.ppermute(x, "cam", moves)


def shards(
    q_tok, k_tok, v_tok, strip_kv, bev_keys, bev_values, bev_list, bev_count, gate_table, timestep
):
    q, k, v = q_tok[0], k_tok[0], v_tok[0]
    smem = pl.BlockSpec(memory_space=pltpu.SMEM)
    vmem = pl.BlockSpec(memory_space=pltpu.VMEM)
    gains = lax.dynamic_index_in_dim(gate_table, timestep[0], 0, keepdims=False)
    to_z = pl.pallas_call(
        pack_z_kernel,
        out_shape=of((PLACES, Z_ROWS, LANES)),
        in_specs=[pl.BlockSpec(memory_space=pltpu.HBM)] * 3,
        scratch_shapes=[pltpu.VMEM((TOK, WIDTH), BF)] * 3 + [pltpu.SemaphoreType.DMA((3,))],
        compiler_params=params(),
        cost_estimate=cost(0, 2 * 6 * TOK * WIDTH, 0),
        name="pack_z",
    )(*(pltpu.with_memory_space_constraint(t, pltpu.HBM) for t in (q, k, v)))
    mine = z_exchange(to_z)
    to_cam = pl.pallas_call(
        pack_cam_kernel,
        out_shape=[of((C_ROWS, GROUP_COLS))] * NY,
        in_specs=[smem] * 2 + [vmem] * 3,
        compiler_params=params(),
        cost_estimate=cost(0, 2 * 6 * TOK * WIDTH, 0),
        name="pack_cam",
    )(bev_list, bev_count, q, bev_keys, bev_values)
    got = [to_cam[0]] + [y_send(to_cam[d], d) for d in range(1, NY)]
    ring = range(CAMS)
    from_left = lax.ppermute(strip_kv[0, 1], "cam", [(c, (c + 1) % CAMS) for c in ring])
    from_right = lax.ppermute(strip_kv[0, 0], "cam", [(c, (c - 1) % CAMS) for c in ring])
    view = pl.pallas_call(
        view_kernel,
        out_shape=of((TOK, WIDTH), F32),
        compiler_params=params(),
        cost_estimate=cost(16 * TOK * 64 * WIDTH, 4 * TOK * WIDTH, TOK * 64 * 24),
        name="view_attention",
    )(q, from_left, from_right)
    to_far = jnp.concatenate([t[:C_Q] for t in got], axis=0)
    far = lax.ppermute(to_far, "cam", [(c, (c + NY) % CAMS) for c in ring])
    mine = after(mine, view, to_far, gains)
    other = lax.ppermute(mine, "seq", [(s, s ^ 1) for s in range(4 * NZ)])
    queries = 3 * NZ * TOK
    v_mine, q_all = pl.pallas_call(
        lay_mine_kernel,
        out_shape=[of((2, V_ROWS, KEYS // 2)), of((queries, LANES))],
        compiler_params=params(),
        cost_estimate=cost(0, 4 * KEYS * LANES, 0),
        name="lay_mine",
    )(mine)
    self_out = pl.pallas_call(
        self_kernel,
        out_shape=of((PLACES, O_ROWS, LANES)),
        scratch_shapes=[
            pltpu.VMEM((2, V_ROWS, KEYS // 2), BF),
            pltpu.VMEM((2, KEYS, BQ), F32),
            pltpu.VMEM((2, 8, BQ), F32),
            pltpu.VMEM((queries, LANES), F32),
        ],
        compiler_params=params(24),
        cost_estimate=cost(16 * queries * KEYS * HALF, 8 * KEYS * LANES, queries * KEYS),
        name="self_attention",
    )(mine, other, v_mine, q_all)
    self_back = z_exchange(self_out)
    far = after(far, self_out)
    layout_out = pl.pallas_call(
        layout_kernel,
        out_shape=[of((TOK, GROUP_COLS))] * NY,
        scratch_shapes=[
            pltpu.VMEM((CAMS, C_Q, GROUP_COLS), BF),
            pltpu.VMEM((CAMS, LANES), jnp.int32),
            pltpu.SMEM((CAMS, LANES), jnp.int32),
            pltpu.SemaphoreType.DMA(()),
        ],
        compiler_params=params(),
        cost_estimate=cost(16 * TOK * 384 * WIDTH, 4 * TOK * WIDTH, TOK * 384 * 24),
        name="layout_attention",
    )(*got, far)
    cam_back = [layout_out[0]] + [y_send(layout_out[d], NY - d) for d in range(1, NY)]
    blended = pl.pallas_call(
        blend_kernel,
        out_shape=of((TOK, WIDTH)),
        scratch_shapes=[pltpu.VMEM((NY, TOK, GROUP_COLS), BF)],
        compiler_params=params(),
        cost_estimate=cost(0, 10 * TOK * WIDTH, 0),
        name="blend",
    )(self_back, *cam_back, view, gains)
    return blended[None]


def solution(mesh):
    return jax.shard_map(
        shards,
        mesh=mesh,
        in_specs=(
            P("cam", "seq", None),
            P("cam", "seq", None),
            P("cam", "seq", None),
            P("cam", None, None, "seq", None),
            P(("cam", "seq"), None),
            P(("cam", "seq"), None),
            P("cam", "seq", None),
            P("cam", "seq"),
            P(),
            P(),
        ),
        out_specs=P("cam", "seq", None),
        check_vma=False,
    )
```

```python
import functools
import math

import jax
import jax.numpy as jnp
from jax import lax
from jax.experimental import pallas as pl
from jax.experimental.pallas import tpu as pltpu
from jax.sharding import PartitionSpec as P

BF = jnp.bfloat16
F32 = jnp.float32
LANES = 128
HALF = 64
LIST = 3
NZ = 8
CAMS = 8
NY = 4
GROUP_PAIRS = 3
GROUP_COLS = GROUP_PAIRS * 128
PLACES = 2 * NZ
TOK = 128
EDGE = 32
WIDTH = 1536
KEYS = 4096
META = 16
BQ = 256
KT = 256
V_ROWS = 80
SCALE = math.log2(math.e) / math.sqrt(HALF)
NT = (((1,), (1,)), ((), ()))
MIB = 2**20

Q_ONE = TOK
KV_TWO = Q_ONE + TOK // 2
Q_TWO = KV_TWO + TOK
Z_ROWS = Q_TWO + TOK // 4
O_ROWS = TOK // 2 + TOK // 4

C_V = TOK
C_Q = 2 * TOK
C_META = 3 * TOK
C_ROWS = C_META + META


def low_lanes(rows):
    return lax.broadcasted_iota(jnp.int32, (rows, LANES), 1) < HALF


def half_turn(x):
    return pltpu.roll(x, HALF, 1)


def side_by_side(a, a_half, b, b_half):
    left = half_turn(a) if a_half else a
    right = b if b_half else half_turn(b)
    return jnp.where(low_lanes(a.shape[0]), left, right)


def folded(x, half):
    n = x.shape[0] // 2
    return side_by_side(x[:n], half, x[n:], half)


def tile(ref, index):
    return ref[:, index * LANES : (index + 1) * LANES]


def params(mib=12):
    return pltpu.CompilerParams(vmem_limit_bytes=mib * MIB)


def pack_z_kernel(q_hbm, k_hbm, v_hbm, out_hbm, q_ref, k_ref, v_ref, out_ref, sems, out_sems):
    half_cols = NZ // 2 * LANES
    copies = []
    for part, at in enumerate((2 * half_cols, 0, half_cols)):
        for i, (a, b) in enumerate(((k_hbm, k_ref), (v_hbm, v_ref), (q_hbm, q_ref))):
            cols = (slice(None), pl.ds(at, half_cols))
            copies.append(pltpu.make_async_copy(a.at[cols], b.at[cols], sems.at[part, i]))
            copies[-1].start()
    sends = []
    for z in range(NZ):
        if z % 4 == 0:
            for copy in copies[:6] if z == 0 else copies[6:]:
                copy.wait()
        at, half = NZ + z // 2, z % 2
        shared = side_by_side(tile(k_ref, at), half, tile(v_ref, at), half)
        q_shared = tile(q_ref, at)
        k, v, q = tile(k_ref, z), tile(v_ref, z), tile(q_ref, z)
        for x in range(2):
            place = 2 * z + x
            out_ref[place, :Q_ONE] = side_by_side(k, x, v, x)
            out_ref[place, Q_ONE:KV_TWO] = folded(q, x)
            out_ref[place, KV_TWO:Q_TWO] = shared
            out_ref[place, Q_TWO:] = folded(q_shared[x * HALF : (x + 1) * HALF], half)
        if z % 4 == 3:
            done = pl.ds(2 * (z - 3), NZ)
            sends.append(
                pltpu.make_async_copy(out_ref.at[done], out_hbm.at[done], out_sems.at[z // 4])
            )
            sends[-1].start()
    for send in sends:
        send.wait()


def pack_cam_kernel(list_ref, count_ref, q_ref, k_ref, v_ref, *outs):
    y = lax.rem(lax.axis_index("cam"), NY)
    lane = lax.broadcasted_iota(jnp.int32, (META, GROUP_COLS), 1)
    uses = jnp.where(lane == LIST, count_ref[0, 0], 0)
    for j in range(LIST):
        uses = jnp.where(lane == j, list_ref[0, 0, j], uses)
    uses = uses.astype(F32).astype(BF)
    for d, out_ref in enumerate(outs):
        cols = pl.ds(pl.multiple_of(lax.rem(y + d, NY) * GROUP_COLS, LANES), GROUP_COLS)
        out_ref[:C_V] = k_ref[:, cols]
        out_ref[C_V:C_Q] = v_ref[:, cols]
        out_ref[C_Q:C_META] = q_ref[:, cols]
        out_ref[C_META:] = uses


def lay_values(ref, v_all):
    for place in range(PLACES):
        cols = slice(place * TOK, (place + 1) * TOK)
        v_all[0, :HALF, cols] = ref[place, :TOK].T[HALF:]
        v_all[1, :HALF, cols] = ref[place, KV_TWO:Q_TWO].T[HALF:]
    v_all[:, HALF:] = jnp.ones((2, V_ROWS - HALF, KEYS // 2), BF)


def lay_mine_kernel(mine_ref, v_all, q_all):
    lay_values(mine_ref, v_all)

    def unfold(q, at):
        n = q.shape[0]
        low, nil = low_lanes(n), jnp.zeros((n, LANES), BF)
        q_all[at : at + n] = jnp.where(low, q, nil)
        q_all[at + n : at + 2 * n] = jnp.where(low, half_turn(q), nil)

    for place in range(PLACES):
        unfold(mine_ref[place, Q_ONE:KV_TWO], place * TOK)
        unfold(mine_ref[place, Q_TWO:], PLACES * TOK + place * HALF)


def self_kernel(mine_ref, other_ref, v_mine, q_all, o_ref, v_other, s_buf, m_buf, o_all):
    both, v_both = (mine_ref, other_ref), (v_mine, v_other)
    lay_values(other_ref, v_other)
    first = PLACES * TOK
    change = first // BQ
    steps = change + change // 2

    def scores(i, slot):
        rows = pl.ds(pl.multiple_of(i // change * KV_TWO, HALF), TOK)
        q = q_all[pl.ds(pl.multiple_of(i * BQ, BQ), BQ)]
        largest = jnp.full((8, BQ), -jnp.inf, F32)
        for t in range(2 * PLACES):
            keys = both[t // PLACES][t % PLACES, rows]
            s = lax.dot_general(keys, q, NT, preferred_element_type=F32)
            s_buf[slot, t * TOK : (t + 1) * TOK] = s
            largest = jnp.maximum(largest, jnp.max(s.reshape(TOK // 8, 8, BQ), axis=0))
        top = jnp.max(largest, axis=0, keepdims=True) * SCALE
        m_buf[slot] = jnp.broadcast_to(top, (8, BQ))

    def values(i, slot):
        top = m_buf[slot][:1]
        total = jnp.zeros((V_ROWS, BQ), F32)
        for t in range(KEYS // KT):
            s = s_buf[slot, t * KT : (t + 1) * KT]
            w = jnp.exp2(s * SCALE - top).astype(BF)
            half, at = divmod(t * KT, KEYS // 2)
            vals = v_both[half][i // change, :, at : at + KT]
            total = total + jnp.dot(vals, w, preferred_element_type=F32)
        out = total[:HALF] / total[HALF : HALF + 1]
        out = jnp.concatenate([out, out], axis=0).T
        o_all[pl.ds(pl.multiple_of(i * BQ, BQ), BQ)] = out

    scores(0, 0)

    def two_steps(j, carry):
        i = 2 * j
        scores(i + 1, 1)
        values(i, 0)
        scores(jnp.minimum(i + 2, steps - 1), 0)
        values(i + 1, 1)
        return carry

    lax.fori_loop(0, steps // 2, two_steps, 0)

    def fold(at, n):
        return jnp.where(low_lanes(n), o_all[at : at + n], o_all[at + n : at + 2 * n]).astype(BF)

    for place in range(PLACES):
        o_ref[place, : TOK // 2] = fold(place * TOK, TOK // 2)
        o_ref[place, TOK // 2 :] = fold(first + place * HALF, TOK // 4)


def attention(q, blocks, allowed=None):
    scores = [lax.dot_general(q, keys, NT, preferred_element_type=F32) for keys, _ in blocks]
    if allowed is not None:
        scores = [jnp.where(ok, s, -1e30) for ok, s in zip(allowed, scores)]
    top = jnp.max(functools.reduce(jnp.maximum, scores), axis=1, keepdims=True) * SCALE
    weights = jnp.concatenate([jnp.exp2(s * SCALE - top).astype(BF) for s in scores], axis=1)
    wide = jnp.concatenate([v for _, v in blocks], axis=0)
    wide = jnp.concatenate([wide, jnp.ones_like(wide)], axis=1)
    total = jnp.dot(weights, wide, preferred_element_type=F32)
    return total[:, :LANES] / total[:, LANES:]


def pair_attention(q, blocks, allowed=None):
    low, nil = low_lanes(TOK), jnp.zeros_like(q)
    both = jnp.concatenate([jnp.where(low, q, nil), jnp.where(low, nil, q)], axis=0)
    out = attention(both, blocks, allowed)
    return jnp.where(low, out[:TOK], out[TOK:])


def view_kernel(q_ref, left_ref, right_ref, out_ref):
    for i in range(WIDTH // LANES):
        cols = slice(i * LANES, (i + 1) * LANES)
        keys = jnp.concatenate([left_ref[0, :, cols], right_ref[0, :, cols]], axis=0)
        vals = jnp.concatenate([left_ref[1, :, cols], right_ref[1, :, cols]], axis=0)
        out_ref[:, cols] = pair_attention(q_ref[:, cols], [(keys, vals)])


def layout_kernel(*refs):
    in_refs, far_ref, o_refs = refs[:NY], refs[NY], refs[NY + 1 : 2 * NY + 1]
    kv_all, uses_vec, uses_ref, sem = refs[2 * NY + 1 :]
    cam = lax.axis_index("cam")
    x_hi, y = cam // NY, lax.rem(cam, NY)
    for d in range(NY):
        uses_vec[d : d + 1] = in_refs[d][C_META:, :LANES].astype(F32)[:1].astype(jnp.int32)
    uses_vec[NY:] = jnp.zeros((NY, LANES), jnp.int32)
    copy = pltpu.make_async_copy(uses_vec, uses_ref, sem)
    copy.start()
    for d in range(NY):
        kv_all[d] = in_refs[d][:C_Q]
        kv_all[NY + d] = far_ref[d * C_Q : (d + 1) * C_Q]
    copy.wait()
    for d in range(NY):
        places, allowed = [], []
        for j in range(LIST):
            e = uses_ref[d, j]
            place = lax.rem(y - lax.rem(e, NY) + NY, NY)
            places.append(jnp.where(e // NY == x_hi, place, place + NY))
            allowed.append(j < uses_ref[d, LIST])
        for p in range(GROUP_PAIRS):
            cols = slice(p * LANES, (p + 1) * LANES)
            blocks = [(kv_all[e, :C_V, cols], kv_all[e, C_V:, cols]) for e in places]
            q = in_refs[d][C_Q:C_META, cols]
            o_refs[d][:, cols] = pair_attention(q, blocks, allowed).astype(BF)


def blend_kernel(self_ref, *refs):
    cam_refs = refs[:NY]
    view_ref, gain_ref, out_ref, cam_all = refs[NY:]
    y = lax.rem(lax.axis_index("cam"), NY)
    for d in range(NY):
        cam_all[lax.rem(y + d, NY)] = cam_refs[d][...]

    def unfolded(x, y, n):
        lower = side_by_side(x, 0, y, 0)
        upper = side_by_side(x, 1, y, 1)
        return jnp.concatenate([lower, upper], axis=0)

    for i in range(WIDTH // LANES):
        cols = slice(i * LANES, (i + 1) * LANES)
        if i < NZ:
            one, two = (self_ref[2 * i + x, : TOK // 2].astype(F32) for x in range(2))
            mine = unfolded(one, two, HALF)
        else:
            z = 2 * (i - NZ)
            parts = []
            for x in range(2):
                one, two = (self_ref[2 * (z + k) + x, TOK // 2 :].astype(F32) for k in range(2))
                parts.append(unfolded(one, two, HALF // 2))
            mine = jnp.concatenate(parts, axis=0)
        at = i % GROUP_PAIRS
        other = cam_all[i // GROUP_PAIRS, :, at * LANES : (at + 1) * LANES].astype(F32)
        blended = gain_ref[0:1, cols] * mine + gain_ref[1:2, cols] * view_ref[:, cols]
        out_ref[:, cols] = (blended + gain_ref[2:3, cols] * other).astype(BF)


def of(shape, dtype=BF):
    return jax.ShapeDtypeStruct(shape, dtype)


def cost(flops, moved, exps):
    return pl.CostEstimate(flops=flops, bytes_accessed=moved, transcendentals=exps)


def after(x, *done):
    return lax.optimization_barrier((x,) + done)[0]


SAME_CORE = [[4 * z + 2 * x + c for z in range(NZ) for x in range(2)] for c in range(2)]


def z_exchange(x):
    return lax.all_to_all(x, "seq", 0, 0, axis_index_groups=SAME_CORE, tiled=True)


def y_send(x, by):
    moves = [(NY * a + b, NY * a + (b + by) % NY) for a in range(2) for b in range(NY)]
    return lax.ppermute(x, "cam", moves)


def shards(
    q_tok, k_tok, v_tok, strip_kv, bev_keys, bev_values, bev_list, bev_count, gate_table, timestep
):
    q, k, v = q_tok[0], k_tok[0], v_tok[0]
    smem = pl.BlockSpec(memory_space=pltpu.SMEM)
    vmem = pl.BlockSpec(memory_space=pltpu.VMEM)
    gains = lax.dynamic_index_in_dim(gate_table, timestep[0], 0, keepdims=False)
    to_z = pl.pallas_call(
        pack_z_kernel,
        out_shape=of((PLACES, Z_ROWS, LANES)),
        in_specs=[pl.BlockSpec(memory_space=pltpu.HBM)] * 3,
        out_specs=pl.BlockSpec(memory_space=pltpu.HBM),
        scratch_shapes=[pltpu.VMEM((TOK, WIDTH), BF)] * 3
        + [pltpu.VMEM((PLACES, Z_ROWS, LANES), BF)]
        + [pltpu.SemaphoreType.DMA((3, 3)), pltpu.SemaphoreType.DMA((2,))],
        compiler_params=params(),
        cost_estimate=cost(0, 2 * 6 * TOK * WIDTH, 0),
        name="pack_z",
    )(*(pltpu.with_memory_space_constraint(t, pltpu.HBM) for t in (q, k, v)))
    mine = z_exchange(to_z)
    to_cam = pl.pallas_call(
        pack_cam_kernel,
        out_shape=[of((C_ROWS, GROUP_COLS))] * NY,
        in_specs=[smem] * 2 + [vmem] * 3,
        compiler_params=params(),
        cost_estimate=cost(0, 2 * 6 * TOK * WIDTH, 0),
        name="pack_cam",
    )(bev_list, bev_count, q, bev_keys, bev_values)
    got = [to_cam[0]] + [y_send(to_cam[d], d) for d in range(1, NY)]
    ring = range(CAMS)
    from_left = lax.ppermute(strip_kv[0, 1], "cam", [(c, (c + 1) % CAMS) for c in ring])
    from_right = lax.ppermute(strip_kv[0, 0], "cam", [(c, (c - 1) % CAMS) for c in ring])
    view = pl.pallas_call(
        view_kernel,
        out_shape=of((TOK, WIDTH), F32),
        compiler_params=params(),
        cost_estimate=cost(16 * TOK * 64 * WIDTH, 4 * TOK * WIDTH, TOK * 64 * 24),
        name="view_attention",
    )(q, from_left, from_right)
    to_far = jnp.concatenate([t[:C_Q] for t in got], axis=0)
    far = lax.ppermute(to_far, "cam", [(c, (c + NY) % CAMS) for c in ring])
    mine = after(mine, view, to_far, gains)
    other = lax.ppermute(mine, "seq", [(s, s ^ 1) for s in range(4 * NZ)])
    queries = 3 * NZ * TOK
    v_mine, q_all = pl.pallas_call(
        lay_mine_kernel,
        out_shape=[of((2, V_ROWS, KEYS // 2)), of((queries, LANES))],
        compiler_params=params(),
        cost_estimate=cost(0, 4 * KEYS * LANES, 0),
        name="lay_mine",
    )(mine)
    self_out = pl.pallas_call(
        self_kernel,
        out_shape=of((PLACES, O_ROWS, LANES)),
        scratch_shapes=[
            pltpu.VMEM((2, V_ROWS, KEYS // 2), BF),
            pltpu.VMEM((2, KEYS, BQ), F32),
            pltpu.VMEM((2, 8, BQ), F32),
            pltpu.VMEM((queries, LANES), F32),
        ],
        compiler_params=params(24),
        cost_estimate=cost(16 * queries * KEYS * HALF, 8 * KEYS * LANES, queries * KEYS),
        name="self_attention",
    )(mine, other, v_mine, q_all)
    self_back = z_exchange(self_out)
    far = after(far, self_out)
    layout_out = pl.pallas_call(
        layout_kernel,
        out_shape=[of((TOK, GROUP_COLS))] * NY,
        scratch_shapes=[
            pltpu.VMEM((CAMS, C_Q, GROUP_COLS), BF),
            pltpu.VMEM((CAMS, LANES), jnp.int32),
            pltpu.SMEM((CAMS, LANES), jnp.int32),
            pltpu.SemaphoreType.DMA(()),
        ],
        compiler_params=params(),
        cost_estimate=cost(16 * TOK * 384 * WIDTH, 4 * TOK * WIDTH, TOK * 384 * 24),
        name="layout_attention",
    )(*got, far)
    cam_back = [layout_out[0]] + [y_send(layout_out[d], NY - d) for d in range(1, NY)]
    blended = pl.pallas_call(
        blend_kernel,
        out_shape=of((TOK, WIDTH)),
        scratch_shapes=[pltpu.VMEM((NY, TOK, GROUP_COLS), BF)],
        compiler_params=params(),
        cost_estimate=cost(0, 10 * TOK * WIDTH, 0),
        name="blend",
    )(self_back, *cam_back, view, gains)
    return blended[None]


def solution(mesh):
    return jax.shard_map(
        shards,
        mesh=mesh,
        in_specs=(
            P("cam", "seq", None),
            P("cam", "seq", None),
            P("cam", "seq", None),
            P("cam", None, None, "seq", None),
            P(("cam", "seq"), None),
            P(("cam", "seq"), None),
            P("cam", "seq", None),
            P("cam", "seq"),
            P(),
            P(),
        ),
        out_specs=P("cam", "seq", None),
        check_vma=False,
    )
```
